128 devices in a mesh: group: 32 (over y, z_hi, x), seq: 4 (over z_lo, core).
Axes of the slice: x: 4, y: 4, z: 4 (z_hi: 2, z_lo: 2; z = z_hi * 2 + z_lo), core: 2. Of those that a mesh axis runs over, the one named last changes fastest.
Arguments:
- queries: bfloat16 [4, 128, 8192], P(None, 'group'), may hold values from -48 to 48
- new_keys: bfloat16 [4, 128, 512], P(None, 'group'), may hold values from -5 to 5
- new_values: bfloat16 [4, 128, 512], P(None, 'group'), may hold values from -24 to 24
- prefix_keys: bfloat16 [64, 16384, 512], P('group', 'seq'), may hold values from -6 to 6
- prefix_values: bfloat16 [64, 16384, 512], P('group', 'seq'), may hold values from -24 to 24
- prefix_block_scales: bfloat16 [64, 128, 8], P('group', 'seq'), may hold values from 0.5 to 2
- suffix_key_pools: bfloat16 [2048, 64, 512], P(('group', 'seq')), may hold values from -6 to 6
- suffix_value_pools: bfloat16 [2048, 64, 512], P(('group', 'seq')), may hold values from -24 to 24
- prefix_home: int32 [64], replicated, may hold values from 0 to 63, as said below
- request_prefix: int32 [128], P('group'), may hold values from 0 to 63, as said below
- suffix_lengths: int32 [128], P('group'), may hold values from 1 to 1024, 98304 in all
- block_table: int32 [128, 4, 4], P('group', 'seq'), may hold values from 0 to 15, as said below
Outputs:
- attended: bfloat16 [4, 128, 8192], P(None, 'group', 'seq')
The draws below stay inside these ranges and needn't reach their ends.
Inputs may be any that keep to these rules, and one draw needn't show every extreme that they name: prefix_home is a permutation: prefix p is stored in row prefix_home[p] of the prefix arrays, so its prefill root is group index prefix_home[p] // 2. `request_prefix`: the root of the prefix of every request of decode group d is d, d - 1, ... or d - 2, counted cyclically over the groups; in every decode group some request's prefix has its root the farthest of these, d - 2. On every device the entries block_table[r, s, :] of its 4 requests form a permutation of its pages.
All inputs are finite; a program needn't handle non-finite values. No bound on the sum of `suffix_lengths` on one device may be relied on, other than what follows from the above.
Results may differ from the reference program's by a relative error of at most 0.017.
Values may be sent and summed in bfloat16 or wider, within the bound.
A program may use at most 192 MiB of HBM per device.

```python
import math
import jax
import jax.numpy as jnp
import numpy as np
from jax import lax

QUERY_HEADS = 64
KEY_VALUE_HEADS = 4
HEAD_SIZE = 128
KVW = 512
DECODE_STEPS = 4
PFX_DEV = 2
PREFIX_COUNT = 64
REQ_DEV = 4
REQUEST_TOTAL = 128
PREFIX_LENGTH = 16384
SCALE_BLOCK = 128
SUFFIX_SLOTS = 1024
PAGE = 64
REACH = 3
SLOC = 256
BLK = 4
PAGES_DEV = 16
PAGES = 2048


def shared_order(key):
    return jax.random.permutation(jax.random.fold_in(key, 101), PREFIX_COUNT).astype(jnp.int32)


def shared_fields(key):
    leading_key = jax.random.fold_in(key, 202)
    gaussian_source = jnp.clip(jax.random.normal(leading_key, (DECODE_STEPS, REQUEST_TOTAL, KEY_VALUE_HEADS, HEAD_SIZE), jnp.float32), -5.0, 5.0)
    return gaussian_source


def draw_prefix_home(key, part):
    home_rows = shared_order(key)
    return home_rows


def draw_request_prefix(key, part):
    home_rows = shared_order(key)
    key = jax.random.fold_in(key, 5)
    owner_of = jnp.argsort(home_rows).astype(jnp.int32)
    request_ids = jnp.arange(REQUEST_TOTAL, dtype=jnp.int32)
    decode_group = request_ids // REQ_DEV
    group_total = PREFIX_COUNT // PFX_DEV
    distance = jax.random.randint(jax.random.fold_in(key, 1), (REQUEST_TOTAL,), 0, REACH, dtype=jnp.int32)
    distance = jnp.where(request_ids % REQ_DEV == 0, REACH - 1, distance)
    slot_index = jax.random.randint(jax.random.fold_in(key, 2), (REQUEST_TOTAL,), 0, PFX_DEV, dtype=jnp.int32)
    root_group = (decode_group - distance) % group_total
    return owner_of[root_group * PFX_DEV + slot_index].astype(jnp.int32)


def draw_block_table(key, part):
    key = jax.random.fold_in(key, 7)
    seq_count = SUFFIX_SLOTS // SLOC
    device_count = REQUEST_TOTAL // REQ_DEV * seq_count
    device_keys = jax.random.split(key, device_count)
    orders = jax.vmap(lambda single: jax.random.permutation(single, PAGES_DEV))(device_keys)
    shaped = orders.reshape(REQUEST_TOTAL // REQ_DEV, seq_count, REQ_DEV, BLK).transpose(0, 2, 1, 3)
    return shaped.reshape(REQUEST_TOTAL, seq_count, BLK).astype(jnp.int32)


def draw_new_keys(key, part):
    gaussian_source = shared_fields(key)
    key_region = gaussian_source
    return key_region.reshape(DECODE_STEPS, REQUEST_TOTAL, KEY_VALUE_HEADS * HEAD_SIZE).astype(jnp.bfloat16)


def draw_queries(key, part):
    gaussian_source = shared_fields(key)
    key = jax.random.fold_in(key, 13)
    decode_groups = QUERY_HEADS // KEY_VALUE_HEADS
    field_layout = (DECODE_STEPS, REQUEST_TOTAL, KEY_VALUE_HEADS, decode_groups, HEAD_SIZE)
    jitter = jnp.clip(jax.random.normal(key, field_layout, jnp.float32), -5.0, 5.0)
    query_field = 0.5 * gaussian_source[:, :, :, None, :] + jitter
    return query_field.reshape(DECODE_STEPS, REQUEST_TOTAL, QUERY_HEADS * HEAD_SIZE).astype(jnp.bfloat16)


def block_scale(stream_key, extent, cuts, least, largest):
    loudness, own = 1.0, jax.random.fold_in(stream_key, 6)
    for position, blocks in cuts:
        steps = jnp.exp(jax.random.uniform(jax.random.fold_in(own, position), (blocks,), jnp.float32, least / len(cuts), largest / len(cuts)))
        loudness = loudness * jnp.repeat(steps, extent[position] // blocks).reshape([-1 if axis == position else 1 for axis in range(len(extent))])
    return loudness


def split_up(count, total, most, slope):
    loads = [(1 << 20) // math.isqrt(standing ** slope) + 1 for standing in range(2, count + 1)]
    surplus, holding = total - most - (count - 1), [1] * (count - 1)
    while surplus > 0:
        movable = [i for i in range(count - 1) if holding[i] < most]
        whole, remaining = sum([loads[i] for i in movable]), surplus
        for i in movable:
            more = min(most - holding[i], max(1, remaining * loads[i] // whole), surplus)
            holding[i] = holding[i] + more
            surplus = surplus - more
    return np.array([most] + holding)


def ragged(stream_key, number_of, total, limit, lean):
    if number_of == 2:
        one = jax.random.randint(stream_key, (), max(1, total - limit), min(limit, total - 1) + 1)
        return jnp.stack([one, total - one])
    lengths = jnp.asarray(split_up(number_of, total, limit, lean), jnp.int32)
    pairs = (number_of - 1) // 2
    donor, receiver = lengths[1:1 + 2 * pairs:2], lengths[2:2 + 2 * pairs:2]
    slack = jnp.minimum(donor - 1, limit - receiver)
    shifted = jax.random.randint(jax.random.fold_in(stream_key, 1), (pairs,), 0, 1 << 20) % (slack + 1)
    lengths = lengths.at[1:1 + 2 * pairs:2].set(donor - shifted).at[2:2 + 2 * pairs:2].set(receiver + shifted)
    return lengths[jax.random.permutation(jax.random.fold_in(stream_key, 2), number_of)]


def scatter_about(key, shape, scale, reach, pieces=(), held_as=jnp.bfloat16):
    values = scale * jax.random.normal(key, shape, jnp.float32)
    if pieces:
        values = values * block_scale(key, shape, pieces, -0.22, 0.18)
    return jnp.clip(values, -reach, reach).astype(held_as)


def setup_inputs(seed: int = 0) -> dict:
    keys = jax.random.split(jax.random.key(seed), 13)
    queries = draw_queries(jax.random.fold_in(keys[12], 71), 0)
    new_keys = draw_new_keys(jax.random.fold_in(keys[12], 71), 0)
    new_values = scatter_about(keys[2], (DECODE_STEPS, REQUEST_TOTAL, KVW), 4.0, 24.0, ((1, 32),))
    prefix_keys = scatter_about(keys[3], (PREFIX_COUNT, PREFIX_LENGTH, KVW), 1.0, 6.0, ((0, 32), (1, 4)))
    prefix_values = scatter_about(keys[4], (PREFIX_COUNT, PREFIX_LENGTH, KVW), 4.0, 24.0, ((0, 32), (1, 4)))
    prefix_block_scales = jnp.clip(jnp.exp(math.log(2.0) - 1.3862944 * jax.random.uniform(keys[5], (PREFIX_COUNT, PREFIX_LENGTH // SCALE_BLOCK, 2 * KEY_VALUE_HEADS), jnp.float32) ** block_scale(keys[5], (PREFIX_COUNT, PREFIX_LENGTH // SCALE_BLOCK, 2 * KEY_VALUE_HEADS), ((0, 32), (1, 4)), -0.2, 0.2)), 0.5, 2.0).astype(jnp.bfloat16)
    suffix_key_pools = scatter_about(keys[6], (PAGES, PAGE, KVW), 1.0, 6.0, ((0, 128),))
    suffix_value_pools = scatter_about(keys[7], (PAGES, PAGE, KVW), 4.0, 24.0, ((0, 128),))
    prefix_home = draw_prefix_home(jax.random.fold_in(keys[12], 71), 0)
    request_prefix = draw_request_prefix(jax.random.fold_in(keys[12], 71), 0)
    suffix_lengths = ragged(keys[10], REQUEST_TOTAL, REQUEST_TOTAL * SUFFIX_SLOTS * 3 // 4, SUFFIX_SLOTS, 0).astype(jnp.int32)
    block_table = draw_block_table(jax.random.fold_in(keys[12], 71), 0)
    return {"queries": queries, "new_keys": new_keys, "new_values": new_values, "prefix_keys": prefix_keys, "prefix_values": prefix_values, "prefix_block_scales": prefix_block_scales, "suffix_key_pools": suffix_key_pools, "suffix_value_pools": suffix_value_pools, "prefix_home": prefix_home, "request_prefix": request_prefix, "suffix_lengths": suffix_lengths, "block_table": block_table}


def widen_block_scales(block_scales, width):
    return jnp.repeat(block_scales.astype(jnp.float32).T, width, axis=1)


def reference(queries, new_keys, new_values, prefix_keys, prefix_values, prefix_block_scales, suffix_key_pools, suffix_value_pools, prefix_home, request_prefix, suffix_lengths, block_table):
    decode_groups = QUERY_HEADS // KEY_VALUE_HEADS
    rows_per_head = DECODE_STEPS * decode_groups
    inv_root = HEAD_SIZE ** -0.5
    ordered_rows = queries.reshape(DECODE_STEPS, REQUEST_TOTAL, KEY_VALUE_HEADS, decode_groups, HEAD_SIZE).transpose(1, 2, 0, 3, 4).reshape(REQUEST_TOTAL, KEY_VALUE_HEADS, rows_per_head, HEAD_SIZE)
    stored_rows = prefix_home[request_prefix]
    seq_count = SUFFIX_SLOTS // SLOC
    request_ids = jnp.arange(REQUEST_TOTAL, dtype=jnp.int32)
    page_base = ((request_ids // REQ_DEV)[:, None] * seq_count + jnp.arange(seq_count, dtype=jnp.int32)[None, :]) * PAGES_DEV
    page_rows = (page_base[:, :, None] + block_table).reshape(REQUEST_TOTAL, seq_count * BLK)
    step_of_row = jnp.arange(rows_per_head, dtype=jnp.int32) // decode_groups
    fresh_visible = jnp.arange(DECODE_STEPS, dtype=jnp.int32)[None, :] <= step_of_row[:, None]
    positions = jnp.arange(SUFFIX_SLOTS, dtype=jnp.int32)

    def scores_of(query_rows, key_entries):
        divided_keys = key_entries.reshape(key_entries.shape[0], KEY_VALUE_HEADS, HEAD_SIZE).astype(jnp.float32)
        return jnp.einsum("hqd,lhd->hql", query_rows.astype(jnp.float32), divided_keys) * inv_root

    def weighted(weights, value_entries):
        divided_values = value_entries.reshape(value_entries.shape[0], KEY_VALUE_HEADS, HEAD_SIZE).astype(jnp.float32)
        return jnp.einsum("hql,lhd->hqd", weights.astype(jnp.float32), divided_values)

    def one_request(request):
        query_rows = ordered_rows[request]
        stored_row = stored_rows[request]
        own_keys = prefix_keys[stored_row]
        own_values = prefix_values[stored_row]
        request_scales = prefix_block_scales[stored_row]
        key_factor = widen_block_scales(request_scales[:, :KEY_VALUE_HEADS], SCALE_BLOCK)[:, None, :]
        value_factor = widen_block_scales(request_scales[:, KEY_VALUE_HEADS:], SCALE_BLOCK)[:, None, :]
        prefix_scores = scores_of(query_rows, own_keys) * key_factor
        page_indices = page_rows[request]
        ending_keys = suffix_key_pools[page_indices].reshape(SUFFIX_SLOTS, KEY_VALUE_HEADS * HEAD_SIZE)
        ending_values = suffix_value_pools[page_indices].reshape(SUFFIX_SLOTS, KEY_VALUE_HEADS * HEAD_SIZE)
        tail_seen = (positions < suffix_lengths[request])[None, None, :]
        tail_scores = jnp.where(tail_seen, scores_of(query_rows, ending_keys), -jnp.inf)
        fresh_scores = jnp.where(fresh_visible[None], scores_of(query_rows, new_keys[:, request]), -jnp.inf)
        highest_score = jnp.maximum(jnp.maximum(jnp.max(prefix_scores, axis=-1), jnp.max(tail_scores, axis=-1)), jnp.max(fresh_scores, axis=-1))
        prefix_exp = jnp.exp(prefix_scores - highest_score[..., None])
        tail_exp = jnp.exp(tail_scores - highest_score[..., None])
        fresh_exp = jnp.exp(fresh_scores - highest_score[..., None])
        weight_total = jnp.sum(prefix_exp, axis=-1) + jnp.sum(tail_exp, axis=-1) + jnp.sum(fresh_exp, axis=-1)
        weighted_value_sum = weighted((prefix_exp * value_factor).astype(jnp.bfloat16), own_values)
        weighted_value_sum = weighted_value_sum + weighted(tail_exp.astype(jnp.bfloat16), ending_values)
        weighted_value_sum = weighted_value_sum + weighted(fresh_exp.astype(jnp.bfloat16), new_values[:, request])
        return weighted_value_sum / weight_total[..., None]

    final_output = lax.map(one_request, request_ids)
    final_output = final_output.reshape(REQUEST_TOTAL, KEY_VALUE_HEADS, DECODE_STEPS, decode_groups, HEAD_SIZE).transpose(2, 0, 1, 3, 4)
    return final_output.reshape(DECODE_STEPS, REQUEST_TOTAL, QUERY_HEADS * HEAD_SIZE).astype(jnp.bfloat16)
```

```python
import functools

import jax
import jax.numpy as jnp
from jax import lax
from jax.experimental import pallas as pl
from jax.experimental.pallas import tpu as pltpu
from jax.sharding import PartitionSpec as P

QUERY_HEADS = 64
KV_HEADS = 4
HEAD = 128
STEPS = 4
GROUP_HEADS = QUERY_HEADS // KV_HEADS
ROWS = STEPS * GROUP_HEADS
REACH = 3
REQS = 4
ENTRIES = REACH * REQS
BLOCK = 128
PAGE = 64
LOG2E = 1.4426950408889634
LOWEST = -1e30
MESH = pl.DeviceIdType.MESH
VMEM = pltpu.VMEM
SMEM = pltpu.SMEM


def places():
    group, count = lax.axis_index("group"), lax.axis_size("group")
    seq = lax.axis_index("seq")
    core, z = lax.rem(seq, 2), seq // 2
    sibling = (group, z * 2 + (1 - core))
    across = (group, (1 - z) * 2 + core)

    def along(steps):
        return (lax.rem(group + count + steps, count), seq)

    return seq, core, z, sibling, across, along


def remote(src, dst, send, recv, device):
    return pltpu.make_async_remote_copy(
        src_ref=src, dst_ref=dst, send_sem=send, recv_sem=recv, device_id=device, device_id_type=MESH
    )


def spread_kernel(prefix_ref, q_ref, all_ref, which_ref, rows, x_send, x_recv, w_send, w_recv,
                  z_send, z_recv, c_send, c_recv):
    seq, core, z, sibling, across, along = places()
    barrier = pltpu.get_barrier_semaphore()
    for device in (sibling, across, along(1), along(2)):
        pl.semaphore_signal(barrier, inc=1, device_id=device, device_id_type=MESH)

    lane = lax.broadcasted_iota(jnp.int32, (8, 128), 1)
    which = jnp.zeros((8, 128), jnp.int32)
    for r in range(REQS):
        which = jnp.where(lane == r, prefix_ref[r], which)
    which_ref[0] = which

    def reorder(i, carry):
        t, c = i // KV_HEADS, lax.rem(i, KV_HEADS)
        for h in range(GROUP_HEADS):
            tile = q_ref[t, :, pl.ds(pl.multiple_of((c * GROUP_HEADS + h) * HEAD, HEAD), HEAD)]
            base = c * ROWS + t * GROUP_HEADS + h
            rows[pl.ds(base, REQS, stride=KV_HEADS * ROWS), :] = tile.astype(jnp.float32)
        return carry

    lax.fori_loop(0, STEPS * KV_HEADS, reorder, 0)
    for r in range(REQS):
        part = rows[r * KV_HEADS * ROWS:(r + 1) * KV_HEADS * ROWS, :]
        all_ref[r] = part.reshape(KV_HEADS, ROWS, HEAD).astype(jnp.bfloat16)

    pl.semaphore_wait(barrier, 4)
    started = []
    for j in (2, 1):
        copy = remote(all_ref.at[seq], all_ref.at[j * REQS + seq], x_send.at[j - 1], x_recv.at[j - 1], along(-j))
        copy.start()
        note = remote(which_ref.at[0], which_ref.at[j], w_send.at[j - 1], w_recv.at[j - 1], along(-j))
        note.start()
        started += [copy, note]
    far = lax.rem(seq + 2, 4)
    onward = []
    for j in (1, 2):
        mine = all_ref.at[j * REQS + seq]
        remote(all_ref.at[seq], mine, x_send.at[j - 1], x_recv.at[j - 1], along(-j)).wait_recv()
        up = remote(mine, mine, z_send.at[j - 1], z_recv.at[j - 1], across)
        up.start()
        over = remote(mine, mine, c_send.at[j - 1], c_recv.at[j - 1], sibling)
        over.start()
        onward += [up, over]
    for j in (1, 2):
        theirs = all_ref.at[j * REQS + far]
        remote(theirs, theirs, z_send.at[j - 1], z_recv.at[j - 1], across).wait_recv()
        over = remote(theirs, theirs, c_send.at[j + 1], c_recv.at[j + 1], sibling)
        over.start()
        onward.append(over)
    near = lax.rem(seq, 2)
    beside = seq + 1 - 2 * near
    for j in (1, 2):
        first = all_ref.at[j * REQS + beside]
        remote(first, first, c_send.at[j - 1], c_recv.at[j - 1], sibling).wait_recv()
        second = all_ref.at[j * REQS + lax.rem(beside + 2, 4)]
        remote(second, second, c_send.at[j + 1], c_recv.at[j + 1], sibling).wait_recv()
        remote(which_ref.at[0], which_ref.at[j], w_send.at[j - 1], w_recv.at[j - 1], along(-j)).wait_recv()
    for copy in started + onward:
        copy.wait_send()


def spread(request_prefix, queries):
    dma = pltpu.SemaphoreType.DMA
    return pl.pallas_call(
        spread_kernel,
        out_shape=(
            jax.ShapeDtypeStruct((ENTRIES, KV_HEADS, ROWS, HEAD), jnp.bfloat16),
            jax.ShapeDtypeStruct((REACH, 8, 128), jnp.int32),
        ),
        in_specs=[pl.BlockSpec(memory_space=SMEM), pl.BlockSpec(memory_space=VMEM)],
        out_specs=(pl.BlockSpec(memory_space=VMEM), pl.BlockSpec(memory_space=VMEM)),
        scratch_shapes=[
            pltpu.VMEM((REQS * KV_HEADS * ROWS, HEAD), jnp.float32),
            dma((2,)), dma((2,)), dma((2,)), dma((2,)), dma((2,)), dma((2,)), dma((4,)), dma((4,)),
        ],
        compiler_params=pltpu.CompilerParams(collective_id=1, has_side_effects=True, vmem_limit_bytes=16 * 2**20),
        name="spread",
    )(request_prefix, queries)


GROUPED = 4
TILE = 512
CHUNK = 1024
TAIL = 128


def attend_kernel(which_ref, home_ref, length_ref, table_ref, q_ref, nk_ref, nv_ref, scale_ref,
                  k_hbm, v_hbm, sk_hbm, sv_hbm, o_ref, st_ref,
                  kbuf, vbuf, ksuf, vsuf, s_a, s_b, kscale, vscale, lcol, fresh, jobs, counts,
                  k_sem, v_sem, p_sem):
    span = k_hbm.shape[1]
    chunks = span // CHUNK
    slots = k_hbm.shape[0]
    local = (table_ref.shape[2]) * PAGE
    me = lax.axis_index("group")
    seq = lax.axis_index("seq")
    f32, bf16 = jnp.float32, jnp.bfloat16

    def page_copies(r, b):
        page = table_ref[r, 0, b]
        place = pl.ds(b * PAGE, PAGE)
        return (
            pltpu.make_async_copy(sk_hbm.at[page], ksuf.at[r, place], p_sem.at[0, r, b]),
            pltpu.make_async_copy(sv_hbm.at[page], vsuf.at[r, place], p_sem.at[1, r, b]),
        )

    def chunk_copy(hbm, buf, sem, s, i):
        place = pl.ds(i * CHUNK, CHUNK)
        return pltpu.make_async_copy(hbm.at[s, place], buf.at[s, place], sem.at[s, i])

    pages = local // PAGE
    for r in range(REQS):
        for b in range(pages):
            for copy in page_copies(r, b):
                copy.start()
    for s in range(slots):
        for i in range(chunks):
            chunk_copy(k_hbm, kbuf, k_sem, s, i).start()
        for i in range(chunks):
            chunk_copy(v_hbm, vbuf, v_sem, s, i).start()

    for s in range(slots):
        counts[s] = 0
    for e in range(ENTRIES):
        row = home_ref[which_ref[e // REQS, 0, e % REQS]]
        s = lax.rem(row, slots)
        at = counts[s]
        jobs[s, at] = e
        counts[s] = at + jnp.where(row // slots == me, 1, 0)

    for s in range(slots):
        x = scale_ref[s].astype(f32)
        for c in range(KV_HEADS):
            kscale[s, c] = jnp.broadcast_to(x[:, c:c + 1] * (HEAD ** -0.5 * LOG2E), kscale.shape[2:])
            vscale[s, c] = jnp.broadcast_to(x[:, KV_HEADS + c:KV_HEADS + c + 1], vscale.shape[2:])

    o_ref[:, pl.ds(REQS, ENTRIES - REQS)] = jnp.zeros((KV_HEADS, ENTRIES - REQS, ROWS, HEAD), bf16)
    lcol[:, pl.ds(REQS, ENTRIES - REQS)] = jnp.full((KV_HEADS, ENTRIES - REQS, ROWS, HEAD), LOWEST, f32)
    st_ref[...] = jnp.full(st_ref.shape, LOWEST, f32)

    eye = lax.broadcasted_iota(jnp.int32, (ROWS, 128), 0) == lax.broadcasted_iota(jnp.int32, (ROWS, 128), 1)

    def as_row(column):
        return jnp.sum(jnp.where(eye, column, 0.0), axis=0, keepdims=True)

    for ref, new in ((ksuf, nk_ref), (vsuf, nv_ref)):
        for u in range(STEPS):
            fresh[u * REQS:(u + 1) * REQS, :] = new[u].astype(f32)
        packed = fresh[...].astype(bf16)
        for r in range(REQS):
            ref[r, local:local + STEPS * REQS, :] = packed
            ref[r, local + STEPS * REQS:, :] = jnp.zeros((TAIL - STEPS * REQS, packed.shape[1]), bf16)
    for r in range(REQS):
        for b in range(pages):
            for copy in page_copies(r, b):
                copy.wait()

    width = local + TAIL
    column = lax.broadcasted_iota(jnp.int32, (ROWS, width), 1)
    step = lax.broadcasted_iota(jnp.int32, (ROWS, width), 0) // GROUP_HEADS
    late = column - local

    def suffix(r, carry):
        length = length_ref[r]
        seen = (column < local) & (seq * local + column < length)
        seen |= (late >= 0) & (late < STEPS * REQS) & (late % REQS == r) & (late // REQS <= step) & (seq == 0)
        for c in range(KV_HEADS):
            lanes = slice(c * HEAD, (c + 1) * HEAD)
            s = lax.dot_general(q_ref[r, c], ksuf[r, :, lanes], (((1,), (1,)), ((), ())),
                                preferred_element_type=f32) * (HEAD ** -0.5 * LOG2E)
            s = jnp.where(seen, s, LOWEST)
            top = jnp.max(s, axis=1, keepdims=True)
            p = jnp.where(seen, jnp.exp2(s - top), 0.0)
            total = jnp.sum(p, axis=1, keepdims=True)
            acc = jnp.dot(p.astype(bf16), vsuf[r, :, lanes], preferred_element_type=f32)
            some = total > 0.0
            total = jnp.where(some, total, 1.0)
            lse = jnp.broadcast_to(jnp.where(some, top + jnp.log2(total), LOWEST), (ROWS, HEAD))
            o_ref[c, r] = (acc / total).astype(bf16)
            lcol[c, r] = lse
            st_ref[c, 0, pl.ds(r, 1), :] = as_row(lse)
        return carry

    lax.fori_loop(0, REQS, suffix, 0)

    per_tile = TILE // BLOCK
    tiles = span // TILE

    def group(s, at, n, first):
        rows = n * ROWS

        def lanes_of(c):
            return pl.ds(pl.multiple_of(c * HEAD, HEAD), HEAD)

        def queries_of(c):
            return jnp.concatenate([q_ref[jobs[s, at + j], c] for j in range(n)], axis=0)

        def score(buf, q, c, t, m):
            k = kbuf[s, t * TILE:(t + 1) * TILE, lanes_of(c)]
            sc = lax.dot_general(q, k, (((1,), (1,)), ((), ())), preferred_element_type=f32)
            for b in range(per_tile):
                part = sc[:, b * BLOCK:(b + 1) * BLOCK] * kscale[s, c, t * per_tile + b:t * per_tile + b + 1, :]
                buf[t * per_tile + b, 0:rows, :] = part
                m = jnp.maximum(m, part)
            return m

        def weigh(buf, top, c, t, total, acc):
            parts = []
            for b in range(per_tile):
                p = jnp.exp2(buf[t * per_tile + b, 0:rows, :] - top)
                total = total + p
                p = p * vscale[s, c, t * per_tile + b:t * per_tile + b + 1, :]
                parts.append(p.astype(bf16))
            v = vbuf[s, t * TILE:(t + 1) * TILE, lanes_of(c)]
            acc = acc + jnp.dot(jnp.concatenate(parts, axis=1), v, preferred_element_type=f32)
            return total, acc

        def row_top(m):
            return jnp.broadcast_to(jnp.max(m, axis=1, keepdims=True), (rows, HEAD))

        def finish(c, top, total, acc):
            total = jnp.broadcast_to(jnp.sum(total, axis=1, keepdims=True), (rows, HEAD))
            lse = top + jnp.log2(total)
            out = acc / total
            for j in range(n):
                e = jobs[s, at + j]
                mine = slice(j * ROWS, (j + 1) * ROWS)
                old = lcol[c, e]
                share = 1.0 / (1.0 + jnp.exp2(old - lse[mine]))
                before = o_ref[c, e].astype(f32)
                o_ref[c, e] = (before + share * (out[mine] - before)).astype(bf16)
                both = jnp.maximum(old, lse[mine]) + jnp.log2(1.0 + jnp.exp2(-jnp.abs(old - lse[mine])))
                st_ref[c, e // REQS, pl.ds(lax.rem(e, REQS), 1), :] = as_row(both)

        def pair(i, carry):
            c1, c2 = 2 * i, 2 * i + 1
            q1, q2 = queries_of(c1), queries_of(c2)
            m1 = jnp.full((rows, BLOCK), LOWEST, f32)
            m2 = m1
            for t in range(tiles):
                m1 = score(s_a, q1, c1, t, m1)
                m2 = score(s_b, q2, c2, t, m2)
            m1, m2 = row_top(m1), row_top(m2)

            @pl.when(first & (i == 0))
            def _():
                for k in range(chunks):
                    chunk_copy(v_hbm, vbuf, v_sem, s, k).wait()

            zero = jnp.zeros((rows, HEAD), f32)
            l1, a1, l2, a2 = zero, zero, zero, zero
            for t in range(tiles):
                l1, a1 = weigh(s_a, m1, c1, t, l1, a1)
                l2, a2 = weigh(s_b, m2, c2, t, l2, a2)
            finish(c1, m1, l1, a1)
            finish(c2, m2, l2, a2)
            return carry

        lax.fori_loop(0, KV_HEADS // 2, pair, 0)

    def one_slot(s, carry):
        for k in range(chunks):
            chunk_copy(k_hbm, kbuf, k_sem, s, k).wait()
        wanted = counts[s]

        def some(i, carry):
            at = i * GROUPED
            left = jnp.minimum(wanted - at, GROUPED)
            for n in range(1, GROUPED + 1):
                @pl.when(left == n)
                def _(n=n):
                    group(s, at, n, i == 0)
            return carry

        lax.fori_loop(0, (wanted + GROUPED - 1) // GROUPED, some, 0)

        @pl.when(wanted == 0)
        def _():
            for k in range(chunks):
                chunk_copy(v_hbm, vbuf, v_sem, s, k).wait()

        return carry

    lax.fori_loop(0, slots, one_slot, 0)


def attend(which, home, lengths, table, q, nk, nv, scales, k, v, sk, sv):
    slots, span, width = k.shape
    local = table.shape[2] * PAGE
    vmem, smem, hbm = (pl.BlockSpec(memory_space=m) for m in (VMEM, SMEM, pl.ANY))
    dma = pltpu.SemaphoreType.DMA
    return pl.pallas_call(
        attend_kernel,
        out_shape=(
            jax.ShapeDtypeStruct((KV_HEADS, ENTRIES, ROWS, HEAD), jnp.bfloat16),
            jax.ShapeDtypeStruct((KV_HEADS, REACH, 8, 128), jnp.float32),
        ),
        in_specs=[smem, smem, smem, smem, vmem, vmem, vmem, vmem, hbm, hbm, hbm, hbm],
        out_specs=(vmem, vmem),
        scratch_shapes=[
            pltpu.VMEM((slots, span, width), jnp.bfloat16),
            pltpu.VMEM((slots, span, width), jnp.bfloat16),
            pltpu.VMEM((REQS, local + TAIL, width), jnp.bfloat16),
            pltpu.VMEM((REQS, local + TAIL, width), jnp.bfloat16),
            pltpu.VMEM((span // BLOCK, GROUPED * ROWS, BLOCK), jnp.float32),
            pltpu.VMEM((span // BLOCK, GROUPED * ROWS, BLOCK), jnp.float32),
            pltpu.VMEM((slots, KV_HEADS, span // BLOCK, 128), jnp.float32),
            pltpu.VMEM((slots, KV_HEADS, span // BLOCK, 128), jnp.float32),
            pltpu.VMEM((KV_HEADS, ENTRIES, ROWS, HEAD), jnp.float32),
            pltpu.VMEM((STEPS * REQS, width), jnp.float32),
            pltpu.SMEM((slots, 16), jnp.int32),
            pltpu.SMEM((slots,), jnp.int32),
            dma((slots, span // CHUNK)), dma((slots, span // CHUNK)), dma((2, REQS, local // PAGE)),
        ],
        compiler_params=pltpu.CompilerParams(vmem_limit_bytes=56 * 2**20),
        name="attend",
    )(which, home, lengths, table, q, nk, nv, scales, k, v, sk, sv)


def gather_kernel(o_ref, st_ref, out_ref, c_o, c_s, z_o, z_s, zr_o, zr_s, x_o, x_s, xr_o, xr_s, rows,
                  c_send, c_recv, z_send, z_recv, x_send, x_recv):
    seq, core, z, sibling, across, along = places()
    f32, bf16 = jnp.float32, jnp.bfloat16
    barrier = pltpu.get_barrier_semaphore()
    for device in (sibling, across, along(-1), along(-2)):
        pl.semaphore_signal(barrier, inc=1, device_id=device, device_id_type=MESH)
    pl.semaphore_wait(barrier, 4)

    def entries(j):
        return pl.ds(j * REQS, REQS)

    def joined(s1, s2):
        gap = s2 - s1
        share = 1.0 / (1.0 + jnp.exp2(gap))
        return share.T, jnp.maximum(s1, s2) + jnp.log2(1.0 + jnp.exp2(-jnp.abs(gap)))

    def mixed(share, i, first, second):
        second = second.astype(f32)
        return second + share[0:ROWS, i:i + 1] * (first.astype(f32) - second)

    order = (2, 1, 0)
    core_copies, waits = {}, []
    for j in order:
        for k in (0, 1):
            head = (1 - core) + 2 * (lax.rem(z + 1, 2) if k == 0 else z)
            core_copies[j, k] = (
                remote(o_ref.at[head, entries(j)], c_o.at[k, entries(j)], c_send.at[0, j, k], c_recv.at[0, j, k], sibling),
                remote(st_ref.at[head, j], c_s.at[k, j], c_send.at[1, j, k], c_recv.at[1, j, k], sibling),
            )
            for copy in core_copies[j, k]:
                copy.start()
                waits.append(copy)
    z_copies = {}
    for j in order:
        for k in (0, 1):
            for copy in core_copies[j, k]:
                copy.wait_recv()
            head = core + 2 * (lax.rem(z + 1, 2) if k == 0 else z)
            share, both = joined(st_ref[head, j], c_s[k, j])
            to_o, to_s = (z_o, z_s) if k == 0 else (x_o, x_s)
            to_s[j] = both
            for i in range(REQS):
                e = j * REQS + i
                to_o[e] = mixed(share, i, o_ref[head, e], c_o[k, e]).astype(bf16)
            if k == 0:
                z_copies[j] = (
                    remote(z_o.at[entries(j)], zr_o.at[entries(j)], z_send.at[0, j], z_recv.at[0, j], across),
                    remote(z_s.at[j], zr_s.at[j], z_send.at[1, j], z_recv.at[1, j], across),
                )
                for copy in z_copies[j]:
                    copy.start()
                    waits.append(copy)
    x_copies = {}
    for j in order:
        for copy in z_copies[j]:
            copy.wait_recv()
        share, both = joined(x_s[j], zr_s[j])
        x_s[j] = both
        for i in range(REQS):
            e = j * REQS + i
            x_o[e] = mixed(share, i, x_o[e], zr_o[e]).astype(bf16)
        if j:
            x_copies[j] = (
                remote(x_o.at[entries(j)], xr_o.at[j - 1], x_send.at[0, j - 1], x_recv.at[0, j - 1], along(j)),
                remote(x_s.at[j], xr_s.at[j - 1], x_send.at[1, j - 1], x_recv.at[1, j - 1], along(j)),
            )
            for copy in x_copies[j]:
                copy.start()
                waits.append(copy)
    for j in (1, 2):
        for copy in x_copies[j]:
            copy.wait_recv()
    share1, both = joined(x_s[0], xr_s[0])
    share2, _ = joined(both, xr_s[1])
    for i in range(REQS):
        part = mixed(share1, i, x_o[i], xr_o[0, i])
        rows[i * ROWS:(i + 1) * ROWS, :] = mixed(share2, i, part, xr_o[1, i])
    for t in range(STEPS):
        for h in range(GROUP_HEADS):
            tile = rows[pl.ds(t * GROUP_HEADS + h, REQS, stride=ROWS), :]
            out_ref[t, :, h * HEAD:(h + 1) * HEAD] = tile.astype(bf16)
    for copy in waits:
        copy.wait_send()


def gather(o, st):
    dma = pltpu.SemaphoreType.DMA
    vmem = pl.BlockSpec(memory_space=VMEM)
    tiles = (ENTRIES, ROWS, HEAD)
    return pl.pallas_call(
        gather_kernel,
        out_shape=jax.ShapeDtypeStruct((STEPS, REQS, GROUP_HEADS * HEAD), jnp.bfloat16),
        in_specs=[vmem, vmem],
        out_specs=vmem,
        scratch_shapes=[
            pltpu.VMEM((2,) + tiles, jnp.bfloat16),
            pltpu.VMEM((2, REACH, 8, 128), jnp.float32),
            pltpu.VMEM(tiles, jnp.bfloat16),
            pltpu.VMEM((REACH, 8, 128), jnp.float32),
            pltpu.VMEM(tiles, jnp.bfloat16),
            pltpu.VMEM((REACH, 8, 128), jnp.float32),
            pltpu.VMEM(tiles, jnp.bfloat16),
            pltpu.VMEM((REACH, 8, 128), jnp.float32),
            pltpu.VMEM((2, REQS, ROWS, HEAD), jnp.bfloat16),
            pltpu.VMEM((2, 8, 128), jnp.float32),
            pltpu.VMEM((REQS * ROWS, HEAD), jnp.float32),
            dma((2, REACH, 2)), dma((2, REACH, 2)), dma((2, REACH)), dma((2, REACH)), dma((2, 2)), dma((2, 2)),
        ],
        compiler_params=pltpu.CompilerParams(collective_id=2, has_side_effects=True, vmem_limit_bytes=16 * 2**20),
        name="gather",
    )(o, st)


def on_device(queries, new_keys, new_values, prefix_keys, prefix_values, prefix_block_scales,
              suffix_key_pools, suffix_value_pools, prefix_home, request_prefix, suffix_lengths, block_table):
    every, which = spread(request_prefix, queries)
    o, st = attend(which, prefix_home, suffix_lengths, block_table, every, new_keys, new_values,
                   prefix_block_scales, prefix_keys, prefix_values, suffix_key_pools, suffix_value_pools)
    return gather(o, st)


def solution(mesh):
    return jax.shard_map(
        on_device,
        mesh=mesh,
        in_specs=(
            P(None, "group", None),
            P(None, "group", None),
            P(None, "group", None),
            P("group", "seq", None),
            P("group", "seq", None),
            P("group", "seq", None),
            P(("group", "seq"), None, None),
            P(("group", "seq"), None, None),
            P(),
            P("group"),
            P("group"),
            P("group", "seq", None),
        ),
        out_specs=P(None, "group", "seq"),
        check_vma=False,
    )
```

```python
import functools

import jax
import jax.numpy as jnp
from jax import lax
from jax.experimental import pallas as pl
from jax.experimental.pallas import tpu as pltpu
from jax.sharding import PartitionSpec as P

QUERY_HEADS = 64
KV_HEADS = 4
HEAD = 128
STEPS = 4
GROUP_HEADS = QUERY_HEADS // KV_HEADS
ROWS = STEPS * GROUP_HEADS
REACH = 3
REQS = 4
ENTRIES = REACH * REQS
BLOCK = 128
PAGE = 64
LOG2E = 1.4426950408889634
LOWEST = -1e30
MESH = pl.DeviceIdType.MESH
VMEM = pltpu.VMEM
SMEM = pltpu.SMEM


def places():
    group, count = lax.axis_index("group"), lax.axis_size("group")
    seq = lax.axis_index("seq")
    core, z = lax.rem(seq, 2), seq // 2
    sibling = (group, z * 2 + (1 - core))
    across = (group, (1 - z) * 2 + core)

    def along(steps):
        return (lax.rem(group + count + steps, count), seq)

    return seq, core, z, sibling, across, along


def remote(src, dst, send, recv, device):
    return pltpu.make_async_remote_copy(
        src_ref=src, dst_ref=dst, send_sem=send, recv_sem=recv, device_id=device, device_id_type=MESH
    )


def in_place(x):
    return pltpu.with_memory_space_constraint(x, pltpu.HBM)


def spread_kernel(prefix_ref, q_hbm, *refs):
    kept = (len(refs) - 14) // 2
    held, (all_ref, which_ref), ready = refs[:kept], refs[kept:kept + 2], refs[kept + 2:2 * kept + 2]
    (own, raw, rows, q_sem, h_sem, x_send, x_recv, w_send, w_recv,
     z_send, z_recv, c_send, c_recv) = refs[2 * kept + 2:]
    seq, core, z, sibling, across, along = places()
    barrier = pltpu.get_barrier_semaphore()
    for device in (sibling, across, along(1), along(2)):
        pl.semaphore_signal(barrier, inc=1, device_id=device, device_id_type=MESH)
    fetch = pltpu.make_async_copy(q_hbm, own, q_sem)
    fetch.start()
    holds = []
    for i in range(kept):
        parts = held[i].shape[0] if held[i].shape[0] == 2 else 1
        for p in range(parts):
            place = pl.ds(p * (held[i].shape[0] // parts), held[i].shape[0] // parts)
            holds.append(pltpu.make_async_copy(held[i].at[place], ready[i].at[place], h_sem.at[i, p]))
    for copy in holds:
        copy.start()

    lane = lax.broadcasted_iota(jnp.int32, (8, 128), 1)
    which = jnp.zeros((8, 128), jnp.int32)
    for r in range(REQS):
        which = jnp.where(lane == r, prefix_ref[r], which)
    which_ref[0] = which

    share = GROUP_HEADS * HEAD

    def lanes_of(c):
        return pl.ds(pl.multiple_of(c * share, share), share)

    pl.semaphore_wait(barrier, 4)
    started, x_copies = [], {}
    for j in (2, 1):
        x_copies[j] = remote(q_hbm.at[:, :, lanes_of(seq)], raw.at[j - 1, :, :, lanes_of(seq)],
                             x_send.at[j - 1], x_recv.at[j - 1], along(-j))
        x_copies[j].start()
    notes = {}
    for j in (2, 1):
        notes[j] = remote(which_ref.at[0], which_ref.at[j], w_send.at[j - 1], w_recv.at[j - 1], along(-j))
        notes[j].start()
        started += [x_copies[j], notes[j]]

    def reorder(source, j, c):
        for t in range(STEPS):
            for h in range(GROUP_HEADS):
                at = pl.ds(pl.multiple_of((c * GROUP_HEADS + h) * HEAD, HEAD), HEAD)
                rows[pl.ds(t * GROUP_HEADS + h, REQS, stride=ROWS), :] = source[t, :, at].astype(jnp.float32)
        for r in range(REQS):
            all_ref[j * REQS + r, c] = rows[r * ROWS:(r + 1) * ROWS, :].astype(jnp.bfloat16)

    fetch.wait()

    def reorder_own(c, carry):
        reorder(own, 0, c)
        return carry

    lax.fori_loop(0, KV_HEADS, reorder_own, 0)

    beside = seq + 1 - 2 * core
    far, corner = lax.rem(seq + 2, 4), lax.rem(beside + 2, 4)

    def passed(j, c, send, recv, device):
        part = raw.at[j - 1, :, :, lanes_of(c)]
        return remote(part, part, send, recv, device)

    for j in (1, 2):
        x_copies[j].wait_recv()
        for copy in (passed(j, seq, z_send.at[j - 1], z_recv.at[j - 1], across),
                     passed(j, seq, c_send.at[j - 1], c_recv.at[j - 1], sibling)):
            copy.start()
            started.append(copy)
        reorder(raw.at[j - 1], j, seq)
    for j in (1, 2):
        passed(j, far, z_send.at[j - 1], z_recv.at[j - 1], across).wait_recv()
        copy = passed(j, far, c_send.at[j + 1], c_recv.at[j + 1], sibling)
        copy.start()
        started.append(copy)
        reorder(raw.at[j - 1], j, far)
        passed(j, beside, c_send.at[j - 1], c_recv.at[j - 1], sibling).wait_recv()
        reorder(raw.at[j - 1], j, beside)
    for j in (1, 2):
        passed(j, corner, c_send.at[j + 1], c_recv.at[j + 1], sibling).wait_recv()
        reorder(raw.at[j - 1], j, corner)
        notes[j].wait_recv()
    for copy in started:
        copy.wait_send()
    for copy in holds:
        copy.wait()


def spread(request_prefix, queries, *arrays):
    dma = pltpu.SemaphoreType.DMA
    in_hbm = pl.BlockSpec(memory_space=pltpu.HBM)
    in_vmem = pl.BlockSpec(memory_space=VMEM)
    return pl.pallas_call(
        spread_kernel,
        out_shape=(
            pltpu.VMEM((ENTRIES, KV_HEADS, ROWS, HEAD), jnp.bfloat16),
            pltpu.VMEM((REACH, 8, 128), jnp.int32),
        ) + tuple(pltpu.VMEM(x.shape, x.dtype) for x in arrays),
        in_specs=[pl.BlockSpec(memory_space=SMEM)] + [in_hbm] * (1 + len(arrays)),
        out_specs=(in_vmem,) * (2 + len(arrays)),
        scratch_shapes=[
            pltpu.VMEM(queries.shape, jnp.bfloat16),
            pltpu.VMEM((2,) + queries.shape, jnp.bfloat16),
            pltpu.VMEM((REQS * ROWS, HEAD), jnp.float32),
            dma, dma((len(arrays), 2)), dma((2,)), dma((2,)), dma((2,)), dma((2,)), dma((2,)), dma((2,)), dma((4,)), dma((4,)),
        ],
        compiler_params=pltpu.CompilerParams(collective_id=1, has_side_effects=True, vmem_limit_bytes=8 * 2**20),
        name="spread",
    )(in_place(request_prefix), in_place(queries), *map(in_place, arrays))


GROUPED = 4
TILE = 512
FRESH = 128


def attend_kernel(which_ref, home_ref, length_ref, table_ref, q_ref, nk_ref, nv_ref, scale_ref,
                  kbuf, vbuf, k_pages, v_pages, o_ref, st_ref,
                  k_new, v_new, s_a, s_b, kscale, vscale, lcol, fresh, jobs, counts):
    slots, span, _ = kbuf.shape
    pages = table_ref.shape[2]
    local = pages * PAGE
    me = lax.axis_index("group")
    seq = lax.axis_index("seq")
    f32, bf16 = jnp.float32, jnp.bfloat16

    for s in range(slots):
        counts[s] = 0
    for e in range(ENTRIES):
        row = home_ref[which_ref[e // REQS, 0, e % REQS]]
        s = lax.rem(row, slots)
        at = counts[s]
        jobs[s, at] = e
        counts[s] = at + jnp.where(row // slots == me, 1, 0)

    blocks = span // BLOCK
    for s in range(slots):
        x = scale_ref[s].astype(f32)
        x = jnp.concatenate([x, jnp.zeros((x.shape[0], 128 - blocks), f32)], axis=1).T[0:blocks]
        for c in range(KV_HEADS):
            kscale[s, c] = jnp.broadcast_to(x[:, c:c + 1] * (HEAD ** -0.5 * LOG2E), kscale.shape[2:])
            vscale[s, c] = jnp.broadcast_to(x[:, KV_HEADS + c:KV_HEADS + c + 1], vscale.shape[2:])

    o_ref[:, pl.ds(REQS, ENTRIES - REQS)] = jnp.zeros((KV_HEADS, ENTRIES - REQS, ROWS, HEAD), bf16)
    lcol[:, pl.ds(REQS, ENTRIES - REQS)] = jnp.full((KV_HEADS, ENTRIES - REQS, ROWS, HEAD), LOWEST, f32)
    st_ref[...] = jnp.full(st_ref.shape, LOWEST, f32)

    eye = lax.broadcasted_iota(jnp.int32, (ROWS, 128), 0) == lax.broadcasted_iota(jnp.int32, (ROWS, 128), 1)

    def as_row(column):
        return jnp.sum(jnp.where(eye, column, 0.0), axis=0, keepdims=True)

    used = STEPS * REQS
    for ref, new in ((k_new, nk_ref), (v_new, nv_ref)):
        for u in range(STEPS):
            fresh[u * REQS:(u + 1) * REQS, :] = new[u].astype(f32)
        ref[0:used, :] = fresh[...].astype(bf16)
        ref[used:, :] = jnp.zeros((FRESH - used, fresh.shape[1]), bf16)

    column = lax.broadcasted_iota(jnp.int32, (ROWS, local), 1)
    lane = lax.broadcasted_iota(jnp.int32, (ROWS, FRESH), 1)
    step = lax.broadcasted_iota(jnp.int32, (ROWS, FRESH), 0) // GROUP_HEADS
    older = (lane < (step + 1) * REQS) & (seq == 0)
    contract = (((1,), (1,)), ((), ()))
    for r in range(REQS):
        seen = column < length_ref[r] - seq * local
        seen_new = older & (lax.rem(lane, REQS) == r)
        page = [table_ref[r, 0, b] for b in range(pages)]
        for c in range(KV_HEADS):
            lanes = slice(c * HEAD, (c + 1) * HEAD)
            k = jnp.concatenate([k_pages[p, :, lanes] for p in page], axis=0)
            v = jnp.concatenate([v_pages[p, :, lanes] for p in page], axis=0)
            q = q_ref[r, c]
            s_old = lax.dot_general(q, k, contract, preferred_element_type=f32) * (HEAD ** -0.5 * LOG2E)
            s_new = lax.dot_general(q, k_new[:, lanes], contract, preferred_element_type=f32) * (HEAD ** -0.5 * LOG2E)
            s_old = jnp.where(seen, s_old, LOWEST)
            s_new = jnp.where(seen_new, s_new, LOWEST)
            top = jnp.maximum(jnp.max(s_old, axis=1, keepdims=True), jnp.max(s_new, axis=1, keepdims=True))
            p_old = jnp.where(seen, jnp.exp2(s_old - top), 0.0)
            p_new = jnp.where(seen_new, jnp.exp2(s_new - top), 0.0)
            total = jnp.sum(p_old, axis=1, keepdims=True) + jnp.sum(p_new, axis=1, keepdims=True)
            acc = jnp.dot(p_old.astype(bf16), v, preferred_element_type=f32)
            acc += jnp.dot(p_new.astype(bf16), v_new[:, lanes], preferred_element_type=f32)
            some = total > 0.0
            total = jnp.where(some, total, 1.0)
            lse = jnp.broadcast_to(jnp.where(some, top + jnp.log2(total), LOWEST), (ROWS, HEAD))
            o_ref[c, r] = (acc / total).astype(bf16)
            lcol[c, r] = lse
            st_ref[c, 0, r:r + 1, :] = as_row(lse)

    per_tile = TILE // BLOCK
    tiles = span // TILE

    def group(s, at, n):
        rows = n * ROWS

        def lanes_of(c):
            return pl.ds(pl.multiple_of(c * HEAD, HEAD), HEAD)

        def queries_of(c):
            return jnp.concatenate([q_ref[jobs[s, at + j], c] for j in range(n)], axis=0)

        def score(buf, q, c, t, m):
            k = kbuf[s, t * TILE:(t + 1) * TILE, lanes_of(c)]
            sc = lax.dot_general(q, k, (((1,), (1,)), ((), ())), preferred_element_type=f32)
            for b in range(per_tile):
                part = sc[:, b * BLOCK:(b + 1) * BLOCK] * kscale[s, c, t * per_tile + b:t * per_tile + b + 1, :]
                buf[t * per_tile + b, 0:rows, :] = part
                m = jnp.maximum(m, part)
            return m

        def weigh(buf, top, c, t, total, acc):
            parts = []
            for b in range(per_tile):
                p = jnp.exp2(buf[t * per_tile + b, 0:rows, :] - top)
                total = total + p
                p = p * vscale[s, c, t * per_tile + b:t * per_tile + b + 1, :]
                parts.append(p.astype(bf16))
            v = vbuf[s, t * TILE:(t + 1) * TILE, lanes_of(c)]
            acc = acc + jnp.dot(jnp.concatenate(parts, axis=1), v, preferred_element_type=f32)
            return total, acc

        def row_top(m):
            return jnp.broadcast_to(jnp.max(m, axis=1, keepdims=True), (rows, HEAD))

        def finish(c, top, total, acc):
            total = jnp.broadcast_to(jnp.sum(total, axis=1, keepdims=True), (rows, HEAD))
            lse = top + jnp.log2(total)
            out = acc / total
            for j in range(n):
                e = jobs[s, at + j]
                mine = slice(j * ROWS, (j + 1) * ROWS)
                old = lcol[c, e]
                share = 1.0 / (1.0 + jnp.exp2(old - lse[mine]))
                before = o_ref[c, e].astype(f32)
                o_ref[c, e] = (before + share * (out[mine] - before)).astype(bf16)
                both = jnp.maximum(old, lse[mine]) + jnp.log2(1.0 + jnp.exp2(-jnp.abs(old - lse[mine])))
                st_ref[c, e // REQS, pl.ds(lax.rem(e, REQS), 1), :] = as_row(both)

        def pair(i, carry):
            c1, c2 = 2 * i, 2 * i + 1
            q1, q2 = queries_of(c1), queries_of(c2)
            m1 = jnp.full((rows, BLOCK), LOWEST, f32)
            m2 = m1
            for t in range(tiles):
                m1 = score(s_a, q1, c1, t, m1)
                m2 = score(s_b, q2, c2, t, m2)
            m1, m2 = row_top(m1), row_top(m2)
            zero = jnp.zeros((rows, HEAD), f32)
            l1, a1, l2, a2 = zero, zero, zero, zero
            for t in range(tiles):
                l1, a1 = weigh(s_a, m1, c1, t, l1, a1)
                l2, a2 = weigh(s_b, m2, c2, t, l2, a2)
            finish(c1, m1, l1, a1)
            finish(c2, m2, l2, a2)
            return carry

        lax.fori_loop(0, KV_HEADS // 2, pair, 0)

    def one_slot(s, carry):
        wanted = counts[s]

        def some(i, carry):
            at = i * GROUPED
            left = jnp.minimum(wanted - at, GROUPED)
            for n in range(1, GROUPED + 1):
                @pl.when(left == n)
                def _(n=n):
                    group(s, at, n)
            return carry

        lax.fori_loop(0, (wanted + GROUPED - 1) // GROUPED, some, 0)
        return carry

    lax.fori_loop(0, slots, one_slot, 0)


def attend(which, home, lengths, table, q, nk, nv, scales, k, v, sk, sv):
    slots, span, width = k.shape
    vmem, smem = (pl.BlockSpec(memory_space=m) for m in (VMEM, SMEM))
    return pl.pallas_call(
        attend_kernel,
        out_shape=(
            pltpu.VMEM((KV_HEADS, ENTRIES, ROWS, HEAD), jnp.bfloat16),
            pltpu.VMEM((KV_HEADS, REACH, 8, 128), jnp.float32),
        ),
        in_specs=[smem] * 4 + [vmem] * 8,
        out_specs=(vmem, vmem),
        scratch_shapes=[
            pltpu.VMEM((FRESH, width), jnp.bfloat16),
            pltpu.VMEM((FRESH, width), jnp.bfloat16),
            pltpu.VMEM((span // BLOCK, GROUPED * ROWS, BLOCK), jnp.float32),
            pltpu.VMEM((span // BLOCK, GROUPED * ROWS, BLOCK), jnp.float32),
            pltpu.VMEM((slots, KV_HEADS, span // BLOCK, 128), jnp.float32),
            pltpu.VMEM((slots, KV_HEADS, span // BLOCK, 128), jnp.float32),
            pltpu.VMEM((KV_HEADS, ENTRIES, ROWS, HEAD), jnp.float32),
            pltpu.VMEM((STEPS * REQS, width), jnp.float32),
            pltpu.SMEM((slots, 16), jnp.int32),
            pltpu.SMEM((slots,), jnp.int32),
        ],
        compiler_params=pltpu.CompilerParams(vmem_limit_bytes=24 * 2**20),
        name="attend",
    )(which, home, lengths, table, q, nk, nv, scales, k, v, sk, sv)


def gather_kernel(o_ref, st_ref, out_ref, c_o, c_s, z_o, z_s, zr_o, zr_s, x_o, x_s, xr_o, xr_s, rows,
                  c_send, c_recv, z_send, z_recv, x_send, x_recv):
    seq, core, z, sibling, across, along = places()
    f32, bf16 = jnp.float32, jnp.bfloat16
    barrier = pltpu.get_barrier_semaphore()
    for device in (sibling, across, along(-1), along(-2)):
        pl.semaphore_signal(barrier, inc=1, device_id=device, device_id_type=MESH)
    pl.semaphore_wait(barrier, 4)

    def entries(j):
        return pl.ds(j * REQS, REQS)

    def joined(s1, s2):
        gap = s2 - s1
        share = 1.0 / (1.0 + jnp.exp2(gap))
        return share.T, jnp.maximum(s1, s2) + jnp.log2(1.0 + jnp.exp2(-jnp.abs(gap)))

    def mixed(share, i, first, second):
        second = second.astype(f32)
        return second + share[0:ROWS, i:i + 1] * (first.astype(f32) - second)

    order = (2, 1, 0)
    core_copies, waits = {}, []
    for j in order:
        for k in (0, 1):
            head = (1 - core) + 2 * (lax.rem(z + 1, 2) if k == 0 else z)
            core_copies[j, k] = (
                remote(o_ref.at[head, entries(j)], c_o.at[k, entries(j)], c_send.at[0, j, k], c_recv.at[0, j, k], sibling),
                remote(st_ref.at[head, j], c_s.at[k, j], c_send.at[1, j, k], c_recv.at[1, j, k], sibling),
            )
            for copy in core_copies[j, k]:
                copy.start()
                waits.append(copy)
    z_copies = {}
    for j in order:
        for k in (0, 1):
            for copy in core_copies[j, k]:
                copy.wait_recv()
            head = core + 2 * (lax.rem(z + 1, 2) if k == 0 else z)
            share, both = joined(st_ref[head, j], c_s[k, j])
            to_o, to_s = (z_o, z_s) if k == 0 else (x_o, x_s)
            to_s[j] = both
            for i in range(REQS):
                e = j * REQS + i
                to_o[e] = mixed(share, i, o_ref[head, e], c_o[k, e]).astype(bf16)
            if k == 0:
                z_copies[j] = (
                    remote(z_o.at[entries(j)], zr_o.at[entries(j)], z_send.at[0, j], z_recv.at[0, j], across),
                    remote(z_s.at[j], zr_s.at[j], z_send.at[1, j], z_recv.at[1, j], across),
                )
                for copy in z_copies[j]:
                    copy.start()
                    waits.append(copy)
    x_copies = {}
    for j in order:
        for copy in z_copies[j]:
            copy.wait_recv()
        share, both = joined(x_s[j], zr_s[j])
        x_s[j] = both
        for i in range(REQS):
            e = j * REQS + i
            x_o[e] = mixed(share, i, x_o[e], zr_o[e]).astype(bf16)
        if j:
            x_copies[j] = (
                remote(x_o.at[entries(j)], xr_o.at[j - 1], x_send.at[0, j - 1], x_recv.at[0, j - 1], along(j)),
                remote(x_s.at[j], xr_s.at[j - 1], x_send.at[1, j - 1], x_recv.at[1, j - 1], along(j)),
            )
            for copy in x_copies[j]:
                copy.start()
                waits.append(copy)
    for j in (1, 2):
        for copy in x_copies[j]:
            copy.wait_recv()
    share1, both = joined(x_s[0], xr_s[0])
    share2, _ = joined(both, xr_s[1])
    for i in range(REQS):
        part = mixed(share1, i, x_o[i], xr_o[0, i])
        rows[i * ROWS:(i + 1) * ROWS, :] = mixed(share2, i, part, xr_o[1, i])
    for t in range(STEPS):
        for h in range(GROUP_HEADS):
            tile = rows[pl.ds(t * GROUP_HEADS + h, REQS, stride=ROWS), :]
            out_ref[t, :, h * HEAD:(h + 1) * HEAD] = tile.astype(bf16)
    for copy in waits:
        copy.wait_send()


def gather(o, st):
    dma = pltpu.SemaphoreType.DMA
    vmem = pl.BlockSpec(memory_space=VMEM)
    tiles = (ENTRIES, ROWS, HEAD)
    return pl.pallas_call(
        gather_kernel,
        out_shape=jax.ShapeDtypeStruct((STEPS, REQS, GROUP_HEADS * HEAD), jnp.bfloat16),
        in_specs=[vmem, vmem],
        out_specs=vmem,
        scratch_shapes=[
            pltpu.VMEM((2,) + tiles, jnp.bfloat16),
            pltpu.VMEM((2, REACH, 8, 128), jnp.float32),
            pltpu.VMEM(tiles, jnp.bfloat16),
            pltpu.VMEM((REACH, 8, 128), jnp.float32),
            pltpu.VMEM(tiles, jnp.bfloat16),
            pltpu.VMEM((REACH, 8, 128), jnp.float32),
            pltpu.VMEM(tiles, jnp.bfloat16),
            pltpu.VMEM((REACH, 8, 128), jnp.float32),
            pltpu.VMEM((2, REQS, ROWS, HEAD), jnp.bfloat16),
            pltpu.VMEM((2, 8, 128), jnp.float32),
            pltpu.VMEM((REQS * ROWS, HEAD), jnp.float32),
            dma((2, REACH, 2)), dma((2, REACH, 2)), dma((2, REACH)), dma((2, REACH)), dma((2, 2)), dma((2, 2)),
        ],
        compiler_params=pltpu.CompilerParams(collective_id=2, has_side_effects=True, vmem_limit_bytes=16 * 2**20),
        name="gather",
    )(o, st)


def on_device(queries, new_keys, new_values, prefix_keys, prefix_values, prefix_block_scales,
              suffix_key_pools, suffix_value_pools, prefix_home, request_prefix, suffix_lengths, block_table):
    scales = jnp.swapaxes(prefix_block_scales, 1, 2)
    every, which, *arrays = spread(request_prefix, queries, new_keys, new_values, scales, prefix_keys, prefix_values,
                                   suffix_key_pools, suffix_value_pools)
    o, st = attend(which, in_place(prefix_home), in_place(suffix_lengths), in_place(block_table), every, *arrays)
    return gather(o, st)


def solution(mesh):
    return jax.shard_map(
        on_device,
        mesh=mesh,
        in_specs=(
            P(None, "group", None),
            P(None, "group", None),
            P(None, "group", None),
            P("group", "seq", None),
            P("group", "seq", None),
            P("group", "seq", None),
            P(("group", "seq"), None, None),
            P(("group", "seq"), None, None),
            P(),
            P("group"),
            P("group"),
            P("group", "seq", None),
        ),
        out_specs=P(None, "group", "seq"),
        check_vma=False,
    )
```

```python
import functools

import jax
import jax.numpy as jnp
from jax import lax
from jax.experimental import pallas as pl
from jax.experimental.pallas import tpu as pltpu
from jax.sharding import PartitionSpec as P

QUERY_HEADS = 64
KV_HEADS = 4
HEAD = 128
STEPS = 4
GROUP_HEADS = QUERY_HEADS // KV_HEADS
ROWS = STEPS * GROUP_HEADS
REACH = 3
X = 4
REQS = 4
ENTRIES = REACH * REQS
BLOCK = 128
PAGE = 64
LOG2E = 1.4426950408889634
LOWEST = -1e30
MESH = pl.DeviceIdType.MESH
VMEM = pltpu.VMEM
SMEM = pltpu.SMEM


def places():
    group, count = lax.axis_index("group"), lax.axis_size("group")
    seq = lax.axis_index("seq")
    core, z = lax.rem(seq, 2), seq // 2
    sibling = (group, z * 2 + (1 - core))
    across = (group, (1 - z) * 2 + core)

    def along(steps):
        passed = (lax.rem(group, X) + X + steps) // X - 1
        past = passed * passed
        return (lax.rem(group + count + steps, count), (z + past - 2 * z * past) * 2 + core)

    return seq, core, z, sibling, across, along


def remote(src, dst, send, recv, device):
    return pltpu.make_async_remote_copy(
        src_ref=src, dst_ref=dst, send_sem=send, recv_sem=recv, device_id=device, device_id_type=MESH
    )


PARTS = 1
FRESH = 128


def row_maker():
    eye = lax.broadcasted_iota(jnp.int32, (ROWS, 128), 0) == lax.broadcasted_iota(jnp.int32, (ROWS, 128), 1)

    def as_row(column):
        return jnp.sum(jnp.where(eye, column, 0.0), axis=0, keepdims=True)

    return as_row


def in_place(x):
    return pltpu.with_memory_space_constraint(x, pltpu.HBM)


def spread_kernel(prefix_ref, length_ref, table_ref, home_ref, q_hbm, k_hbm, v_hbm, kp_hbm, vp_hbm,
                  scale_ref, nk_ref, nv_ref, all_ref, which_ref, own_o, own_l, own_st, k_held, v_held, kscale, vscale,
                  own, raw, rows, k_pages, v_pages, k_new, v_new, fresh, q_sem, h_sem, p_sem, x_send, x_recv,
                  w_send, w_recv, z_send, z_recv, c_send, c_recv, d_send, d_recv):
    seq, core, z, sibling, across, along = places()
    barrier = pltpu.get_barrier_semaphore()
    for device in (sibling, across, along(1), along(2)):
        pl.semaphore_signal(barrier, inc=1, device_id=device, device_id_type=MESH)
    fetch = pltpu.make_async_copy(q_hbm, own, q_sem)
    fetch.start()
    page_copies = [pltpu.make_async_copy(kp_hbm, k_pages, p_sem.at[0]), pltpu.make_async_copy(vp_hbm, v_pages, p_sem.at[1])]
    holds = []
    for i, (src, dst) in enumerate(((k_hbm, k_held), (v_hbm, v_held))):
        holds += [pltpu.make_async_copy(src.at[p], dst.at[p], h_sem.at[i, p]) for p in range(src.shape[0])]
    for copy in page_copies:
        copy.start()

    lane = lax.broadcasted_iota(jnp.int32, (8, 128), 1)
    which = jnp.zeros((8, 128), jnp.int32)
    for r in range(REQS):
        which = jnp.where(lane == r, prefix_ref[r], which)
    which_ref[0] = which
    homes = jnp.zeros((8, 128), jnp.int32)
    for p in range(home_ref.shape[0]):
        homes = jnp.where(lane == p, home_ref[p], homes)

    share = GROUP_HEADS * HEAD

    def lanes_of(c):
        return pl.ds(pl.multiple_of(c * share, share), share)

    pl.semaphore_wait(barrier, 4)
    part = STEPS // PARTS
    order = [(j, p) for p in range(PARTS) for j in (2, 1)]
    arrivals = [(j, p) for p in range(PARTS) for j in (1, 2)]
    started, x_copies = [], {}
    for j, p in order:
        steps = pl.ds(p * part, part)
        there = lanes_of(along(-j)[1])
        x_copies[j, p] = remote(q_hbm.at[steps, :, there], raw.at[j - 1, steps, :, there],
                                x_send.at[j - 1, p], x_recv.at[j - 1, p], along(-j))
        x_copies[j, p].start()
        started.append(x_copies[j, p])
    notes = {}
    for j in (2, 1):
        notes[j] = remote(which_ref.at[0], which_ref.at[j], w_send.at[j - 1], w_recv.at[j - 1], along(-j))
        notes[j].start()
        started.append(notes[j])
    which_ref[REACH] = homes

    def reorder(source, j, c, p):
        for t in range(p * part, (p + 1) * part):
            for h in range(GROUP_HEADS):
                at = pl.ds(pl.multiple_of((c * GROUP_HEADS + h) * HEAD, HEAD), HEAD)
                rows[pl.ds(t * GROUP_HEADS + h, REQS, stride=ROWS), :] = source[t, :, at].astype(jnp.float32)
        lo, hi = p * part * GROUP_HEADS, (p + 1) * part * GROUP_HEADS
        for r in range(REQS):
            all_ref[j * REQS + r, c, lo:hi, :] = rows[r * ROWS + lo:r * ROWS + hi, :].astype(jnp.bfloat16)

    fetch.wait()
    for copy in holds:
        copy.start()

    def reorder_own(c, carry):
        for p in range(PARTS):
            reorder(own, 0, c, p)
        return carry

    lax.fori_loop(0, KV_HEADS, reorder_own, 0)

    f32, bf16 = jnp.float32, jnp.bfloat16
    used, pages = STEPS * REQS, table_ref.shape[2]
    local = pages * PAGE
    for ref, new in ((k_new, nk_ref), (v_new, nv_ref)):
        for u in range(STEPS):
            fresh[u * REQS:(u + 1) * REQS, :] = new[u].astype(f32)
        ref[0:used, :] = fresh[...].astype(bf16)
        ref[used:, :] = jnp.zeros((FRESH - used, fresh.shape[1]), bf16)
    column = lax.broadcasted_iota(jnp.int32, (ROWS, local), 1)
    lane = lax.broadcasted_iota(jnp.int32, (ROWS, FRESH), 1)
    step = lax.broadcasted_iota(jnp.int32, (ROWS, FRESH), 0) // GROUP_HEADS
    older = (lane < (step + 1) * REQS) & (seq == 0)
    contract = (((1,), (1,)), ((), ()))
    as_row = row_maker()

    def suffix(r):
        seen = column < length_ref[r] - seq * local
        seen_new = older & (lax.rem(lane, REQS) == r)
        page = [table_ref[r, 0, b] for b in range(pages)]
        for c in range(KV_HEADS):
            lanes = slice(c * HEAD, (c + 1) * HEAD)
            k = jnp.concatenate([k_pages[p, :, lanes] for p in page], axis=0)
            v = jnp.concatenate([v_pages[p, :, lanes] for p in page], axis=0)
            q = all_ref[r, c]
            s_old = lax.dot_general(q, k, contract, preferred_element_type=f32) * (HEAD ** -0.5 * LOG2E)
            s_new = lax.dot_general(q, k_new[:, lanes], contract, preferred_element_type=f32) * (HEAD ** -0.5 * LOG2E)
            parts = [jnp.where(seen[:, i:i + FRESH], s_old[:, i:i + FRESH], LOWEST) for i in range(0, local, FRESH)]
            parts.append(jnp.where(seen_new, s_new, LOWEST))
            top = jnp.max(functools.reduce(jnp.maximum, parts), axis=1, keepdims=True)
            top = jnp.broadcast_to(top, (ROWS, FRESH))
            shown = [seen[:, i:i + FRESH] for i in range(0, local, FRESH)] + [seen_new]
            parts = [jnp.where(show, jnp.exp2(part - top), 0.0) for show, part in zip(shown, parts)]
            total = jnp.sum(functools.reduce(jnp.add, parts), axis=1, keepdims=True)
            total = jnp.broadcast_to(total, (ROWS, HEAD))
            acc = jnp.dot(jnp.concatenate(parts[:-1], axis=1).astype(bf16), v, preferred_element_type=f32)
            acc += jnp.dot(parts[-1].astype(bf16), v_new[:, lanes], preferred_element_type=f32)
            some = total > 0.0
            total = jnp.where(some, total, 1.0)
            lse = jnp.where(some, top + jnp.log2(total), LOWEST)
            own_o[c, r] = (acc / total).astype(bf16)
            own_l[c, r] = lse
            own_st[c, r:r + 1, :] = as_row(lse)

    blocks = k_held.shape[1] // BLOCK
    for s in range(k_held.shape[0]):
        x = scale_ref[s].astype(f32)
        x = jnp.concatenate([x, jnp.zeros((x.shape[0], 128 - blocks), f32)], axis=1).T[0:blocks]
        for c in range(KV_HEADS):
            kscale[s, c] = jnp.broadcast_to(x[:, c:c + 1] * (HEAD ** -0.5 * LOG2E), kscale.shape[2:])
            vscale[s, c] = jnp.broadcast_to(x[:, KV_HEADS + c:KV_HEADS + c + 1], vscale.shape[2:])
    for c in range(KV_HEADS):
        own_st[c] = jnp.full(own_st.shape[1:], LOWEST, f32)
    for copy in page_copies:
        copy.wait()
    for r in (0, 1):
        suffix(r)

    beside = seq + 1 - 2 * core
    far, corner = lax.rem(seq + 2, 4), lax.rem(beside + 2, 4)

    def passed(j, p, c, send, recv, device):
        piece = raw.at[j - 1, pl.ds(p * part, part), :, lanes_of(c)]
        return remote(piece, piece, send.at[j - 1, p], recv.at[j - 1, p], device)

    for j, p in arrivals:
        passed(j, p, seq, x_send, x_recv, along(-j)).wait_recv()
        for copy in (passed(j, p, seq, z_send, z_recv, across), passed(j, p, seq, c_send, c_recv, sibling)):
            copy.start()
            started.append(copy)
    for j, p in arrivals:
        reorder(raw.at[j - 1], j, seq, p)
    for r in (2, 3):
        suffix(r)
    for j, p in arrivals:
        passed(j, p, far, z_send, z_recv, across).wait_recv()
        copy = passed(j, p, far, d_send, d_recv, sibling)
        copy.start()
        started.append(copy)
    for j, p in arrivals:
        reorder(raw.at[j - 1], j, far, p)
    for j, p in arrivals:
        passed(j, p, beside, c_send, c_recv, sibling).wait_recv()
        reorder(raw.at[j - 1], j, beside, p)
    for j, p in arrivals:
        passed(j, p, corner, d_send, d_recv, sibling).wait_recv()
        reorder(raw.at[j - 1], j, corner, p)
    for j in (1, 2):
        notes[j].wait_recv()
    for copy in started:
        copy.wait_send()
    for copy in holds:
        copy.wait()


def spread(request_prefix, lengths, table, home, queries, keys, values, key_pages, value_pages, scales, new_keys, new_values):
    dma = pltpu.SemaphoreType.DMA
    smem, vmem, hbm = (pl.BlockSpec(memory_space=m) for m in (SMEM, VMEM, pltpu.HBM))
    bf16, f32 = jnp.bfloat16, jnp.float32
    width = keys.shape[-1]
    operands = (request_prefix, lengths, table, home, queries, keys, values, key_pages, value_pages,
                scales, new_keys, new_values)
    splat = (keys.shape[0], KV_HEADS, keys.shape[1] // BLOCK, 128)
    return pl.pallas_call(
        spread_kernel,
        out_shape=(
            pltpu.VMEM((ENTRIES, KV_HEADS, ROWS, HEAD), bf16),
            pltpu.VMEM((REACH + 1, 8, 128), jnp.int32),
            pltpu.VMEM((KV_HEADS, REQS, ROWS, HEAD), bf16),
            pltpu.VMEM((KV_HEADS, REQS, ROWS, HEAD), f32),
            pltpu.VMEM((KV_HEADS, 8, 128), f32),
            pltpu.VMEM(keys.shape, bf16),
            pltpu.VMEM(values.shape, bf16),
            pltpu.VMEM(splat, f32),
            pltpu.VMEM(splat, f32),
        ),
        in_specs=[smem] * 4 + [hbm] * 5 + [vmem] * 3,
        out_specs=(vmem,) * 9,
        scratch_shapes=[
            pltpu.VMEM(queries.shape, bf16),
            pltpu.VMEM((2,) + queries.shape, bf16),
            pltpu.VMEM((REQS * ROWS, HEAD), f32),
            pltpu.VMEM(key_pages.shape, bf16),
            pltpu.VMEM(value_pages.shape, bf16),
            pltpu.VMEM((FRESH, width), bf16),
            pltpu.VMEM((FRESH, width), bf16),
            pltpu.VMEM((STEPS * REQS, width), f32),
            dma, dma((2, 2)), dma((2,)), dma((2, PARTS)), dma((2, PARTS)), dma((2,)), dma((2,)),
            dma((2, PARTS)), dma((2, PARTS)), dma((2, PARTS)), dma((2, PARTS)), dma((2, PARTS)), dma((2, PARTS)),
        ],
        compiler_params=pltpu.CompilerParams(collective_id=1, has_side_effects=True, vmem_limit_bytes=14 * 2**20),
        name="spread",
    )(*map(in_place, operands))


GROUPED = 6
TILE = 256


def attend_kernel(which_ref, q_ref, own_o, own_l, own_st, kscale, vscale, kbuf, vbuf, o_ref, st_ref,
                  s_buf, jobs, counts):
    slots, span, _ = kbuf.shape
    me = lax.axis_index("group")
    f32, bf16 = jnp.float32, jnp.bfloat16

    for s in range(slots):
        counts[s] = 0
    for e in range(ENTRIES):
        row = which_ref[REACH, 0, which_ref[e // REQS, 0, e % REQS]]
        s = lax.rem(row, slots)
        at = counts[s]
        jobs[s, at] = e
        counts[s] = at + jnp.where(row // slots == me, 1, 0)

    o_ref[:, pl.ds(REQS, ENTRIES - REQS)] = jnp.zeros((KV_HEADS, ENTRIES - REQS, ROWS, HEAD), bf16)
    st_ref[...] = jnp.full(st_ref.shape, LOWEST, f32)

    as_row = row_maker()

    for c in range(KV_HEADS):
        for r in range(REQS):
            o_ref[c, r] = own_o[c, r]
        st_ref[c, 0] = own_st[c]

    per_tile = TILE // BLOCK
    tiles = span // TILE

    def group(s, at, n):
        rows = n * ROWS

        def lanes_of(c):
            return pl.ds(pl.multiple_of(c * HEAD, HEAD), HEAD)

        def queries_of(c):
            return jnp.concatenate([q_ref[jobs[s, at + j], c] for j in range(n)], axis=0)

        def score(buf, q, c, t, m):
            k = kbuf[s, t * TILE:(t + 1) * TILE, lanes_of(c)]
            sc = lax.dot_general(q, k, (((1,), (1,)), ((), ())), preferred_element_type=f32)
            for b in range(per_tile):
                part = sc[:, b * BLOCK:(b + 1) * BLOCK] * kscale[s, c, t * per_tile + b:t * per_tile + b + 1, :]
                buf[t * per_tile + b, 0:rows, :] = part
                m = jnp.maximum(m, part)
            return m

        def weigh(buf, top, c, t, total, acc):
            parts = []
            for b in range(per_tile):
                p = jnp.exp2(buf[t * per_tile + b, 0:rows, :] - top)
                total = total + p
                p = p * vscale[s, c, t * per_tile + b:t * per_tile + b + 1, :]
                parts.append(p.astype(bf16))
            v = vbuf[s, t * TILE:(t + 1) * TILE, lanes_of(c)]
            acc = acc + jnp.dot(jnp.concatenate(parts, axis=1), v, preferred_element_type=f32)
            return total, acc

        def row_top(m):
            return jnp.broadcast_to(jnp.max(m, axis=1, keepdims=True), (rows, HEAD))

        def finish(c, top, total, acc):
            total = jnp.broadcast_to(jnp.sum(total, axis=1, keepdims=True), (rows, HEAD))
            lse = top + jnp.log2(total)
            out = acc / total
            for j in range(n):
                e = jobs[s, at + j]
                mine = slice(j * ROWS, (j + 1) * ROWS)
                old = jnp.where(e < REQS, own_l[c, jnp.minimum(e, REQS - 1)], LOWEST)
                share = 1.0 / (1.0 + jnp.exp2(old - lse[mine]))
                before = o_ref[c, e].astype(f32)
                o_ref[c, e] = (before + share * (out[mine] - before)).astype(bf16)
                both = jnp.maximum(old, lse[mine]) + jnp.log2(1.0 + jnp.exp2(-jnp.abs(old - lse[mine])))
                st_ref[c, e // REQS, pl.ds(lax.rem(e, REQS), 1), :] = as_row(both)

        def weigh_and_score(c, top, following):
            q = queries_of(following) if following is not None else None
            m = jnp.full((rows, BLOCK), LOWEST, f32)
            total = jnp.zeros((rows, HEAD), f32)
            acc = jnp.zeros((rows, HEAD), f32)
            for t in range(tiles):
                total, acc = weigh(s_buf, top, c, t, total, acc)
                if following is not None:
                    m = score(s_buf, q, following, t, m)
            finish(c, top, total, acc)
            return row_top(m)

        q = queries_of(0)
        m = jnp.full((rows, BLOCK), LOWEST, f32)
        for t in range(tiles):
            m = score(s_buf, q, 0, t, m)
        top = lax.fori_loop(0, KV_HEADS - 1, lambda c, top: weigh_and_score(c, top, c + 1), row_top(m))
        weigh_and_score(KV_HEADS - 1, top, None)

    def one_slot(s, carry):
        wanted = counts[s]

        def some(i, carry):
            at = i * GROUPED
            left = jnp.minimum(wanted - at, GROUPED)
            for n in range(1, GROUPED + 1):
                @pl.when(left == n)
                def _(n=n):
                    group(s, at, n)
            return carry

        lax.fori_loop(0, (wanted + GROUPED - 1) // GROUPED, some, 0)
        return carry

    lax.fori_loop(0, slots, one_slot, 0)


def attend(which, q, own_o, own_l, own_st, key_scales, value_scales, k, v):
    slots, span, width = k.shape
    vmem, smem = (pl.BlockSpec(memory_space=m) for m in (VMEM, SMEM))
    return pl.pallas_call(
        attend_kernel,
        out_shape=(
            pltpu.VMEM((KV_HEADS, ENTRIES, ROWS, HEAD), jnp.bfloat16),
            pltpu.VMEM((KV_HEADS, REACH, 8, 128), jnp.float32),
        ),
        in_specs=[smem] + [vmem] * 8,
        out_specs=(vmem, vmem),
        scratch_shapes=[
            pltpu.VMEM((span // BLOCK, GROUPED * ROWS, BLOCK), jnp.float32),
            pltpu.SMEM((slots, 16), jnp.int32),
            pltpu.SMEM((slots,), jnp.int32),
        ],
        compiler_params=pltpu.CompilerParams(vmem_limit_bytes=24 * 2**20),
        name="attend",
    )(which, q, own_o, own_l, own_st, key_scales, value_scales, k, v)


def gather_kernel(o_ref, st_ref, out_ref, c_o, c_s, z_o, z_s, zr_o, zr_s, x_o, x_s, xr_o, xr_s, rows,
                  c_send, c_recv, z_send, z_recv, x_send, x_recv):
    seq, core, z, sibling, across, along = places()
    f32, bf16 = jnp.float32, jnp.bfloat16
    barrier = pltpu.get_barrier_semaphore()
    for device in (sibling, across, along(-1), along(-2)):
        pl.semaphore_signal(barrier, inc=1, device_id=device, device_id_type=MESH)
    pl.semaphore_wait(barrier, 4)

    def entries(j):
        return pl.ds(j * REQS, REQS)

    def joined(s1, s2):
        gap = s2 - s1
        share = 1.0 / (1.0 + jnp.exp2(gap))
        return share.T, jnp.maximum(s1, s2) + jnp.log2(1.0 + jnp.exp2(-jnp.abs(gap)))

    def mixed(share, i, first, second):
        second = second.astype(f32)
        return second + share[0:ROWS, i:i + 1] * (first.astype(f32) - second)

    order = (2, 1, 0)

    def kept(j):
        return along(j)[1] if j else seq

    def given(j):
        return lax.rem(kept(j) + 2, 4)

    core_copies, waits = {}, []
    for j in order:
        for k in (0, 1):
            head = (given(j) if k == 0 else kept(j)) + 1 - 2 * core
            core_copies[j, k] = (
                remote(o_ref.at[head, entries(j)], c_o.at[k, entries(j)], c_send.at[0, j, k], c_recv.at[0, j, k], sibling),
                remote(st_ref.at[head, j], c_s.at[k, j], c_send.at[1, j, k], c_recv.at[1, j, k], sibling),
            )
            for copy in core_copies[j, k]:
                copy.start()
                waits.append(copy)
    z_copies = {}
    for j in order:
        for k in (0, 1):
            for copy in core_copies[j, k]:
                copy.wait_recv()
            head = given(j) if k == 0 else kept(j)
            share, both = joined(st_ref[head, j], c_s[k, j])
            to_o, to_s = (z_o, z_s) if k == 0 else (x_o, x_s)
            to_s[j] = both
            for i in range(REQS):
                e = j * REQS + i
                to_o[e] = mixed(share, i, o_ref[head, e], c_o[k, e]).astype(bf16)
            if k == 0:
                z_copies[j] = (
                    remote(z_o.at[entries(j)], zr_o.at[entries(j)], z_send.at[0, j], z_recv.at[0, j], across),
                    remote(z_s.at[j], zr_s.at[j], z_send.at[1, j], z_recv.at[1, j], across),
                )
                for copy in z_copies[j]:
                    copy.start()
                    waits.append(copy)
    x_copies = {}
    for j in order:
        for copy in z_copies[j]:
            copy.wait_recv()
        share, both = joined(x_s[j], zr_s[j])
        x_s[j] = both
        for i in range(REQS):
            e = j * REQS + i
            x_o[e] = mixed(share, i, x_o[e], zr_o[e]).astype(bf16)
        if j:
            x_copies[j] = (
                remote(x_o.at[entries(j)], xr_o.at[j - 1], x_send.at[0, j - 1], x_recv.at[0, j - 1], along(j)),
                remote(x_s.at[j], xr_s.at[j - 1], x_send.at[1, j - 1], x_recv.at[1, j - 1], along(j)),
            )
            for copy in x_copies[j]:
                copy.start()
                waits.append(copy)
    for j in (1, 2):
        for copy in x_copies[j]:
            copy.wait_recv()
    share1, both = joined(x_s[0], xr_s[0])
    share2, _ = joined(both, xr_s[1])
    for i in range(REQS):
        part = mixed(share1, i, x_o[i], xr_o[0, i])
        rows[i * ROWS:(i + 1) * ROWS, :] = mixed(share2, i, part, xr_o[1, i])
    for t in range(STEPS):
        for h in range(GROUP_HEADS):
            tile = rows[pl.ds(t * GROUP_HEADS + h, REQS, stride=ROWS), :]
            out_ref[t, :, h * HEAD:(h + 1) * HEAD] = tile.astype(bf16)
    for copy in waits:
        copy.wait_send()


def gather(o, st):
    dma = pltpu.SemaphoreType.DMA
    vmem = pl.BlockSpec(memory_space=VMEM)
    tiles = (ENTRIES, ROWS, HEAD)
    return pl.pallas_call(
        gather_kernel,
        out_shape=jax.ShapeDtypeStruct((STEPS, REQS, GROUP_HEADS * HEAD), jnp.bfloat16),
        in_specs=[vmem, vmem],
        out_specs=vmem,
        scratch_shapes=[
            pltpu.VMEM((2,) + tiles, jnp.bfloat16),
            pltpu.VMEM((2, REACH, 8, 128), jnp.float32),
            pltpu.VMEM(tiles, jnp.bfloat16),
            pltpu.VMEM((REACH, 8, 128), jnp.float32),
            pltpu.VMEM(tiles, jnp.bfloat16),
            pltpu.VMEM((REACH, 8, 128), jnp.float32),
            pltpu.VMEM(tiles, jnp.bfloat16),
            pltpu.VMEM((REACH, 8, 128), jnp.float32),
            pltpu.VMEM((2, REQS, ROWS, HEAD), jnp.bfloat16),
            pltpu.VMEM((2, 8, 128), jnp.float32),
            pltpu.VMEM((REQS * ROWS, HEAD), jnp.float32),
            dma((2, REACH, 2)), dma((2, REACH, 2)), dma((2, REACH)), dma((2, REACH)), dma((2, 2)), dma((2, 2)),
        ],
        compiler_params=pltpu.CompilerParams(collective_id=2, has_side_effects=True, vmem_limit_bytes=16 * 2**20),
        name="gather",
    )(o, st)


def on_device(queries, new_keys, new_values, prefix_keys, prefix_values, prefix_block_scales,
              suffix_key_pools, suffix_value_pools, prefix_home, request_prefix, suffix_lengths, block_table):
    scales = jnp.swapaxes(prefix_block_scales, 1, 2)
    every, which, own_o, own_l, own_st, keys, values, key_scales, value_scales = spread(
        request_prefix, suffix_lengths, block_table, prefix_home, queries, prefix_keys, prefix_values,
        suffix_key_pools, suffix_value_pools, scales, new_keys, new_values)
    o, st = attend(which, every, own_o, own_l, own_st, key_scales, value_scales, keys, values)
    return gather(o, st)


def solution(mesh):
    return jax.shard_map(
        on_device,
        mesh=mesh,
        in_specs=(
            P(None, "group", None),
            P(None, "group", None),
            P(None, "group", None),
            P("group", "seq", None),
            P("group", "seq", None),
            P("group", "seq", None),
            P(("group", "seq"), None, None),
            P(("group", "seq"), None, None),
            P(),
            P("group"),
            P("group"),
            P("group", "seq", None),
        ),
        out_specs=P(None, "group", "seq"),
        check_vma=False,
    )
```

```python
import functools

import jax
import jax.numpy as jnp
from jax import lax
from jax.experimental import pallas as pl
from jax.experimental.pallas import tpu as pltpu
from jax.sharding import PartitionSpec as P

QUERY_HEADS = 64
KV_HEADS = 4
HEAD = 128
STEPS = 4
GROUP_HEADS = QUERY_HEADS // KV_HEADS
ROWS = STEPS * GROUP_HEADS
REACH = 3
X = 4
REQS = 4
ENTRIES = REACH * REQS
BLOCK = 128
PAGE = 64
LOG2E = 1.4426950408889634
LOWEST = -1e30
MESH = pl.DeviceIdType.MESH
VMEM = pltpu.VMEM
SMEM = pltpu.SMEM


def places():
    group, count = lax.axis_index("group"), lax.axis_size("group")
    seq = lax.axis_index("seq")
    core, z = lax.rem(seq, 2), seq // 2
    sibling = (group, z * 2 + (1 - core))
    across = (group, (1 - z) * 2 + core)

    def along(steps):
        passed = (lax.rem(group, X) + X + steps) // X - 1
        past = passed * passed
        return (lax.rem(group + count + steps, count), (z + past - 2 * z * past) * 2 + core)

    return seq, core, z, sibling, across, along


def remote(src, dst, send, recv, device):
    return pltpu.make_async_remote_copy(
        src_ref=src, dst_ref=dst, send_sem=send, recv_sem=recv, device_id=device, device_id_type=MESH
    )


PARTS = 1
FRESH = 128


def row_maker():
    eye = lax.broadcasted_iota(jnp.int32, (ROWS, 128), 0) == lax.broadcasted_iota(jnp.int32, (ROWS, 128), 1)

    def as_row(column):
        return jnp.sum(jnp.where(eye, column, 0.0), axis=0, keepdims=True)

    return as_row


def in_place(x):
    return pltpu.with_memory_space_constraint(x, pltpu.HBM)


def spread_kernel(prefix_hbm, length_hbm, table_hbm, home_hbm, scale_hbm, nk_hbm, nv_hbm,
                  q_hbm, k_hbm, v_hbm, kp_hbm, vp_hbm, all_ref, table_out, own_o, own_l, own_st, k_held, v_held, kscale, vscale,
                  prefix_ref, length_ref, table_ref, home_ref, scale_ref, nk_ref, nv_ref, s_sem,
                  own, raw, which_ref, rows, k_pages, v_pages, k_new, v_new, fresh, q_sem, h_sem, p_sem, x_send, x_recv,
                  w_send, w_recv, z_send, z_recv, c_send, c_recv, d_send, d_recv):
    seq, core, z, sibling, across, along = places()
    barrier = pltpu.get_barrier_semaphore()
    for device in (sibling, across, along(1), along(2)):
        pl.semaphore_signal(barrier, inc=1, device_id=device, device_id_type=MESH)
    fetch = pltpu.make_async_copy(q_hbm, own, q_sem)
    fetch.start()
    small = [pltpu.make_async_copy(src, dst, s_sem.at[i]) for i, (src, dst) in enumerate((
        (prefix_hbm, prefix_ref), (home_hbm, home_ref), (length_hbm, length_ref), (table_hbm, table_ref),
        (scale_hbm, scale_ref), (nk_hbm, nk_ref), (nv_hbm, nv_ref)))]
    for copy in small:
        copy.start()
    page_copies = [pltpu.make_async_copy(kp_hbm, k_pages, p_sem.at[0]), pltpu.make_async_copy(vp_hbm, v_pages, p_sem.at[1])]
    holds = []
    for i, (src, dst) in enumerate(((k_hbm, k_held), (v_hbm, v_held))):
        holds += [pltpu.make_async_copy(src.at[p], dst.at[p], h_sem.at[i, p]) for p in range(src.shape[0])]
    for copy in page_copies:
        copy.start()

    share = GROUP_HEADS * HEAD

    def lanes_of(c):
        return pl.ds(pl.multiple_of(c * share, share), share)

    fetch.wait()
    pl.semaphore_wait(barrier, 4)
    part = STEPS // PARTS
    order = [(j, p) for p in range(PARTS) for j in (2, 1)]
    arrivals = [(j, p) for p in range(PARTS) for j in (1, 2)]
    started, x_copies = [], {}
    for j, p in order:
        steps = pl.ds(p * part, part)
        there = lanes_of(along(-j)[1])
        x_copies[j, p] = remote(own.at[steps, :, there], raw.at[j - 1, steps, :, there],
                                x_send.at[j - 1, p], x_recv.at[j - 1, p], along(-j))
        x_copies[j, p].start()
        started.append(x_copies[j, p])
    for copy in small:
        copy.wait()
    lane = lax.broadcasted_iota(jnp.int32, (8, 128), 1)
    which = jnp.zeros((8, 128), jnp.int32)
    for r in range(REQS):
        which = jnp.where(lane == r, prefix_ref[r], which)
    which_ref[0] = which
    homes = jnp.zeros((8, 128), jnp.int32)
    for p in range(home_ref.shape[0]):
        homes = jnp.where(lane == p, home_ref[p], homes)
    notes = {}
    for j in (2, 1):
        notes[j] = remote(which_ref.at[0], which_ref.at[j], w_send.at[j - 1], w_recv.at[j - 1], along(-j))
        notes[j].start()
        started.append(notes[j])

    def reorder(source, j, c, p):
        for t in range(p * part, (p + 1) * part):
            for h in range(GROUP_HEADS):
                at = pl.ds(pl.multiple_of((c * GROUP_HEADS + h) * HEAD, HEAD), HEAD)
                rows[pl.ds(t * GROUP_HEADS + h, REQS, stride=ROWS), :] = source[t, :, at].astype(jnp.float32)
        lo, hi = p * part * GROUP_HEADS, (p + 1) * part * GROUP_HEADS
        for r in range(REQS):
            all_ref[j * REQS + r, c, lo:hi, :] = rows[r * ROWS + lo:r * ROWS + hi, :].astype(jnp.bfloat16)

    for copy in holds:
        copy.start()

    def reorder_own(c, carry):
        for p in range(PARTS):
            reorder(own, 0, c, p)
        return carry

    lax.fori_loop(0, KV_HEADS, reorder_own, 0)

    f32, bf16 = jnp.float32, jnp.bfloat16
    used, pages = STEPS * REQS, table_ref.shape[2]
    local = pages * PAGE
    for ref, new in ((k_new, nk_ref), (v_new, nv_ref)):
        for u in range(STEPS):
            fresh[u * REQS:(u + 1) * REQS, :] = new[u].astype(f32)
        ref[0:used, :] = fresh[...].astype(bf16)
        ref[used:, :] = jnp.zeros((FRESH - used, fresh.shape[1]), bf16)
    column = lax.broadcasted_iota(jnp.int32, (ROWS, local), 1)
    lane = lax.broadcasted_iota(jnp.int32, (ROWS, FRESH), 1)
    step = lax.broadcasted_iota(jnp.int32, (ROWS, FRESH), 0) // GROUP_HEADS
    older = (lane < (step + 1) * REQS) & (seq == 0)
    contract = (((1,), (1,)), ((), ()))
    as_row = row_maker()

    def suffix(r):
        seen = column < length_ref[r] - seq * local
        seen_new = older & (lax.rem(lane, REQS) == r)
        page = [table_ref[r, 0, b] for b in range(pages)]
        for c in range(KV_HEADS):
            lanes = slice(c * HEAD, (c + 1) * HEAD)
            k = jnp.concatenate([k_pages[p, :, lanes] for p in page], axis=0)
            v = jnp.concatenate([v_pages[p, :, lanes] for p in page], axis=0)
            q = all_ref[r, c]
            s_old = lax.dot_general(q, k, contract, preferred_element_type=f32) * (HEAD ** -0.5 * LOG2E)
            s_new = lax.dot_general(q, k_new[:, lanes], contract, preferred_element_type=f32) * (HEAD ** -0.5 * LOG2E)
            parts = [jnp.where(seen[:, i:i + FRESH], s_old[:, i:i + FRESH], LOWEST) for i in range(0, local, FRESH)]
            parts.append(jnp.where(seen_new, s_new, LOWEST))
            top = jnp.max(functools.reduce(jnp.maximum, parts), axis=1, keepdims=True)
            top = jnp.broadcast_to(top, (ROWS, FRESH))
            shown = [seen[:, i:i + FRESH] for i in range(0, local, FRESH)] + [seen_new]
            parts = [jnp.where(show, jnp.exp2(part - top), 0.0) for show, part in zip(shown, parts)]
            total = jnp.sum(functools.reduce(jnp.add, parts), axis=1, keepdims=True)
            total = jnp.broadcast_to(total, (ROWS, HEAD))
            acc = jnp.dot(jnp.concatenate(parts[:-1], axis=1).astype(bf16), v, preferred_element_type=f32)
            acc += jnp.dot(parts[-1].astype(bf16), v_new[:, lanes], preferred_element_type=f32)
            some = total > 0.0
            total = jnp.where(some, total, 1.0)
            lse = jnp.where(some, top + jnp.log2(total), LOWEST)
            own_o[c, r] = (acc / total).astype(bf16)
            own_l[c, r] = lse
            own_st[c, r:r + 1, :] = as_row(lse)

    blocks = k_held.shape[1] // BLOCK
    for s in range(k_held.shape[0]):
        x = scale_ref[s].astype(f32)
        x = jnp.concatenate([x, jnp.zeros((x.shape[0], 128 - blocks), f32)], axis=1).T[0:blocks]
        for c in range(KV_HEADS):
            kscale[s, c] = jnp.broadcast_to(x[:, c:c + 1] * (HEAD ** -0.5 * LOG2E), kscale.shape[2:])
            vscale[s, c] = jnp.broadcast_to(x[:, KV_HEADS + c:KV_HEADS + c + 1], vscale.shape[2:])
    for c in range(KV_HEADS):
        own_st[c] = jnp.full(own_st.shape[1:], LOWEST, f32)
    for copy in page_copies:
        copy.wait()
    for r in (0, 1, 2):
        suffix(r)

    beside = seq + 1 - 2 * core
    far, corner = lax.rem(seq + 2, 4), lax.rem(beside + 2, 4)

    def passed(j, p, c, send, recv, device):
        piece = raw.at[j - 1, pl.ds(p * part, part), :, lanes_of(c)]
        return remote(piece, piece, send.at[j - 1, p], recv.at[j - 1, p], device)

    for j, p in arrivals:
        passed(j, p, seq, x_send, x_recv, along(-j)).wait_recv()
        for copy in (passed(j, p, seq, z_send, z_recv, across), passed(j, p, seq, c_send, c_recv, sibling)):
            copy.start()
            started.append(copy)
    for j, p in arrivals:
        reorder(raw.at[j - 1], j, seq, p)
    suffix(3)
    for j, p in arrivals:
        passed(j, p, far, z_send, z_recv, across).wait_recv()
        copy = passed(j, p, far, d_send, d_recv, sibling)
        copy.start()
        started.append(copy)
    for j, p in arrivals:
        reorder(raw.at[j - 1], j, far, p)
    for j, p in arrivals:
        passed(j, p, beside, c_send, c_recv, sibling).wait_recv()
        reorder(raw.at[j - 1], j, beside, p)
    for j, p in arrivals:
        passed(j, p, corner, d_send, d_recv, sibling).wait_recv()
        reorder(raw.at[j - 1], j, corner, p)
    for j in (1, 2):
        notes[j].wait_recv()
    row = lax.broadcasted_iota(jnp.int32, (8, 128), 0)
    for j in range(REACH):
        homes = jnp.where(row == j, which_ref[j], homes)
    table_out[...] = homes
    for copy in started:
        copy.wait_send()
    for copy in holds:
        copy.wait()


def spread(request_prefix, lengths, table, home, queries, keys, values, key_pages, value_pages, scales, new_keys, new_values):
    dma = pltpu.SemaphoreType.DMA
    vmem, hbm = (pl.BlockSpec(memory_space=m) for m in (VMEM, pltpu.HBM))
    bf16, f32 = jnp.bfloat16, jnp.float32
    width = keys.shape[-1]
    small = (request_prefix, lengths, table, home)
    operands = small + (scales, new_keys, new_values, queries, keys, values, key_pages, value_pages)
    splat = (keys.shape[0], KV_HEADS, keys.shape[1] // BLOCK, 128)
    return pl.pallas_call(
        spread_kernel,
        out_shape=(
            pltpu.VMEM((ENTRIES, KV_HEADS, ROWS, HEAD), bf16),
            pltpu.VMEM((8, 128), jnp.int32),
            pltpu.VMEM((KV_HEADS, REQS, ROWS, HEAD), bf16),
            pltpu.VMEM((KV_HEADS, REQS, ROWS, HEAD), f32),
            pltpu.VMEM((KV_HEADS, 8, 128), f32),
            pltpu.VMEM(keys.shape, bf16),
            pltpu.VMEM(values.shape, bf16),
            pltpu.VMEM(splat, f32),
            pltpu.VMEM(splat, f32),
        ),
        in_specs=[hbm] * len(operands),
        out_specs=(vmem,) * 9,
        scratch_shapes=[pltpu.SMEM(x.shape, x.dtype) for x in small] + [
            pltpu.VMEM(scales.shape, bf16),
            pltpu.VMEM(new_keys.shape, bf16),
            pltpu.VMEM(new_values.shape, bf16),
            dma((7,)),
            pltpu.VMEM(queries.shape, bf16),
            pltpu.VMEM((2,) + queries.shape, bf16),
            pltpu.VMEM((REACH, 8, 128), jnp.int32),
            pltpu.VMEM((REQS * ROWS, HEAD), f32),
            pltpu.VMEM(key_pages.shape, bf16),
            pltpu.VMEM(value_pages.shape, bf16),
            pltpu.VMEM((FRESH, width), bf16),
            pltpu.VMEM((FRESH, width), bf16),
            pltpu.VMEM((STEPS * REQS, width), f32),
            dma, dma((2, 2)), dma((2,)), dma((2, PARTS)), dma((2, PARTS)), dma((2,)), dma((2,)),
            dma((2, PARTS)), dma((2, PARTS)), dma((2, PARTS)), dma((2, PARTS)), dma((2, PARTS)), dma((2, PARTS)),
        ],
        compiler_params=pltpu.CompilerParams(collective_id=1, has_side_effects=True, vmem_limit_bytes=14 * 2**20),
        name="spread",
    )(*map(in_place, operands))


GROUPED = 6
TILE = 256


def attend_kernel(which_ref, q_ref, own_o, own_l, own_st, kscale, vscale, kbuf, vbuf, o_ref, st_ref,
                  s_buf, jobs, counts):
    slots, span, _ = kbuf.shape
    me = lax.axis_index("group")
    f32, bf16 = jnp.float32, jnp.bfloat16

    found = [jnp.int32(0)] * slots
    for e in range(ENTRIES):
        row = which_ref[REACH, which_ref[e // REQS, e % REQS]]
        for s in range(slots):
            jobs[s, found[s]] = e
            found[s] += jnp.where(row == me * slots + s, 1, 0)
    for s in range(slots):
        counts[s] = found[s]

    o_ref[:, pl.ds(REQS, ENTRIES - REQS)] = jnp.zeros((KV_HEADS, ENTRIES - REQS, ROWS, HEAD), bf16)
    st_ref[...] = jnp.full(st_ref.shape, LOWEST, f32)

    as_row = row_maker()

    for c in range(KV_HEADS):
        for r in range(REQS):
            o_ref[c, r] = own_o[c, r]
        st_ref[c, 0] = own_st[c]

    per_tile = TILE // BLOCK
    tiles = span // TILE

    def group(s, at, n):
        rows = n * ROWS

        def lanes_of(c):
            return pl.ds(pl.multiple_of(c * HEAD, HEAD), HEAD)

        def queries_of(c):
            return jnp.concatenate([q_ref[jobs[s, at + j], c] for j in range(n)], axis=0)

        def score(buf, q, c, t, m):
            k = kbuf[s, t * TILE:(t + 1) * TILE, lanes_of(c)]
            sc = lax.dot_general(q, k, (((1,), (1,)), ((), ())), preferred_element_type=f32)
            for b in range(per_tile):
                part = sc[:, b * BLOCK:(b + 1) * BLOCK] * kscale[s, c, t * per_tile + b:t * per_tile + b + 1, :]
                buf[t * per_tile + b, 0:rows, :] = part
                m = jnp.maximum(m, part)
            return m

        def weigh(buf, top, c, t, total, acc):
            parts = []
            for b in range(per_tile):
                p = jnp.exp2(buf[t * per_tile + b, 0:rows, :] - top)
                total = total + p
                p = p * vscale[s, c, t * per_tile + b:t * per_tile + b + 1, :]
                parts.append(p.astype(bf16))
            v = vbuf[s, t * TILE:(t + 1) * TILE, lanes_of(c)]
            acc = acc + jnp.dot(jnp.concatenate(parts, axis=1), v, preferred_element_type=f32)
            return total, acc

        def row_top(m):
            return jnp.broadcast_to(jnp.max(m, axis=1, keepdims=True), (rows, HEAD))

        def finish(c, top, total, acc):
            total = jnp.broadcast_to(jnp.sum(total, axis=1, keepdims=True), (rows, HEAD))
            lse = top + jnp.log2(total)
            out = acc / total
            for j in range(n):
                e = jobs[s, at + j]
                mine = slice(j * ROWS, (j + 1) * ROWS)
                old = jnp.where(e < REQS, own_l[c, jnp.minimum(e, REQS - 1)], LOWEST)
                share = 1.0 / (1.0 + jnp.exp2(old - lse[mine]))
                before = o_ref[c, e].astype(f32)
                o_ref[c, e] = (before + share * (out[mine] - before)).astype(bf16)
                both = jnp.maximum(old, lse[mine]) + jnp.log2(1.0 + jnp.exp2(-jnp.abs(old - lse[mine])))
                st_ref[c, e // REQS, pl.ds(lax.rem(e, REQS), 1), :] = as_row(both)

        def weigh_and_score(c, top, following):
            q = queries_of(following) if following is not None else None
            m = jnp.full((rows, BLOCK), LOWEST, f32)
            total = jnp.zeros((rows, HEAD), f32)
            acc = jnp.zeros((rows, HEAD), f32)
            for t in range(tiles):
                total, acc = weigh(s_buf, top, c, t, total, acc)
                if following is not None:
                    m = score(s_buf, q, following, t, m)
            finish(c, top, total, acc)
            return row_top(m)

        q = queries_of(0)
        m = jnp.full((rows, BLOCK), LOWEST, f32)
        for t in range(tiles):
            m = score(s_buf, q, 0, t, m)
        top = lax.fori_loop(0, KV_HEADS - 1, lambda c, top: weigh_and_score(c, top, c + 1), row_top(m))
        weigh_and_score(KV_HEADS - 1, top, None)

    def one_slot(s, carry):
        wanted = counts[s]

        def some(i, carry):
            at = i * GROUPED
            left = jnp.minimum(wanted - at, GROUPED)
            for n in range(1, GROUPED + 1):
                @pl.when(left == n)
                def _(n=n):
                    group(s, at, n)
            return carry

        lax.fori_loop(0, (wanted + GROUPED - 1) // GROUPED, some, 0)
        return carry

    lax.fori_loop(0, slots, one_slot, 0)


def attend(which, q, own_o, own_l, own_st, key_scales, value_scales, k, v):
    slots, span, width = k.shape
    vmem, smem = (pl.BlockSpec(memory_space=m) for m in (VMEM, SMEM))
    return pl.pallas_call(
        attend_kernel,
        out_shape=(
            pltpu.VMEM((KV_HEADS, ENTRIES, ROWS, HEAD), jnp.bfloat16),
            pltpu.VMEM((KV_HEADS, REACH, 8, 128), jnp.float32),
        ),
        in_specs=[smem] + [vmem] * 8,
        out_specs=(vmem, vmem),
        scratch_shapes=[
            pltpu.VMEM((span // BLOCK, GROUPED * ROWS, BLOCK), jnp.float32),
            pltpu.SMEM((slots, 16), jnp.int32),
            pltpu.SMEM((slots,), jnp.int32),
        ],
        compiler_params=pltpu.CompilerParams(vmem_limit_bytes=24 * 2**20),
        name="attend",
    )(which, q, own_o, own_l, own_st, key_scales, value_scales, k, v)


HALVES = 2


def gather_kernel(o_ref, st_ref, out_ref, c_o, c_s, z_o, z_s, zr_o, zr_s, x_o, x_s, xr_o, xr_s, rows,
                  c_send, c_recv, z_send, z_recv, x_send, x_recv):
    seq, core, z, sibling, across, along = places()
    f32, bf16 = jnp.float32, jnp.bfloat16
    barrier = pltpu.get_barrier_semaphore()
    for device in (sibling, across, along(-1), along(-2)):
        pl.semaphore_signal(barrier, inc=1, device_id=device, device_id_type=MESH)
    pl.semaphore_wait(barrier, 4)

    def entries(j):
        return pl.ds(j * REQS, REQS)

    half = REQS // HALVES

    def half_of(j, p):
        return pl.ds(j * REQS + p * half, half)

    def joined(s1, s2):
        gap = s2 - s1
        share = 1.0 / (1.0 + jnp.exp2(gap))
        return share.T, jnp.maximum(s1, s2) + jnp.log2(1.0 + jnp.exp2(-jnp.abs(gap)))

    def mixed(share, i, first, second):
        second = second.astype(f32)
        return second + share[0:ROWS, i:i + 1] * (first.astype(f32) - second)

    order = (2, 1, 0)

    def kept(j):
        return along(j)[1] if j else seq

    def given(j):
        return lax.rem(kept(j) + 2, 4)

    core_copies, waits = {}, []
    for k in (0, 1):
        for j in order:
            head = (given(j) if k == 0 else kept(j)) + 1 - 2 * core
            core_copies[j, k] = (
                remote(o_ref.at[head, entries(j)], c_o.at[k, entries(j)], c_send.at[0, j, k], c_recv.at[0, j, k], sibling),
                remote(st_ref.at[head, j], c_s.at[k, j], c_send.at[1, j, k], c_recv.at[1, j, k], sibling),
            )
            for copy in core_copies[j, k]:
                copy.start()
                waits.append(copy)
    z_copies = {}
    for k in (0, 1):
        for j in order:
            for copy in core_copies[j, k]:
                copy.wait_recv()
            head = given(j) if k == 0 else kept(j)
            share, both = joined(st_ref[head, j], c_s[k, j])
            to_o, to_s = (z_o, z_s) if k == 0 else (x_o, x_s)
            to_s[j] = both
            if k == 0:
                z_copies[j] = [remote(z_s.at[j], zr_s.at[j], z_send.at[HALVES, j], z_recv.at[HALVES, j], across)]
                z_copies[j][0].start()
            for p in range(HALVES):
                for i in range(p * half, (p + 1) * half):
                    e = j * REQS + i
                    to_o[e] = mixed(share, i, o_ref[head, e], c_o[k, e]).astype(bf16)
                if k == 0:
                    copy = remote(z_o.at[half_of(j, p)], zr_o.at[half_of(j, p)], z_send.at[p, j], z_recv.at[p, j], across)
                    copy.start()
                    z_copies[j].append(copy)
            if k == 0:
                waits += z_copies[j]
    x_copies = {}
    for j in order:
        z_copies[j][0].wait_recv()
        share, both = joined(x_s[j], zr_s[j])
        x_s[j] = both
        if j:
            x_copies[j] = [remote(x_s.at[j], xr_s.at[j - 1], x_send.at[HALVES, j - 1], x_recv.at[HALVES, j - 1], along(j))]
            x_copies[j][0].start()
        for p in range(HALVES):
            z_copies[j][1 + p].wait_recv()
            for i in range(p * half, (p + 1) * half):
                e = j * REQS + i
                x_o[e] = mixed(share, i, x_o[e], zr_o[e]).astype(bf16)
            if j:
                copy = remote(x_o.at[half_of(j, p)], xr_o.at[j - 1, pl.ds(p * half, half)],
                              x_send.at[p, j - 1], x_recv.at[p, j - 1], along(j))
                copy.start()
                x_copies[j].append(copy)
        if j:
            waits += x_copies[j]
    for j in (1, 2):
        for copy in x_copies[j]:
            copy.wait_recv()
    share1, both = joined(x_s[0], xr_s[0])
    share2, _ = joined(both, xr_s[1])
    for i in range(REQS):
        part = mixed(share1, i, x_o[i], xr_o[0, i])
        rows[i * ROWS:(i + 1) * ROWS, :] = mixed(share2, i, part, xr_o[1, i])
    for t in range(STEPS):
        for h in range(GROUP_HEADS):
            tile = rows[pl.ds(t * GROUP_HEADS + h, REQS, stride=ROWS), :]
            out_ref[t, :, h * HEAD:(h + 1) * HEAD] = tile.astype(bf16)
    for copy in waits:
        copy.wait_send()


def gather(o, st):
    dma = pltpu.SemaphoreType.DMA
    vmem = pl.BlockSpec(memory_space=VMEM)
    tiles = (ENTRIES, ROWS, HEAD)
    return pl.pallas_call(
        gather_kernel,
        out_shape=jax.ShapeDtypeStruct((STEPS, REQS, GROUP_HEADS * HEAD), jnp.bfloat16),
        in_specs=[vmem, vmem],
        out_specs=vmem,
        scratch_shapes=[
            pltpu.VMEM((2,) + tiles, jnp.bfloat16),
            pltpu.VMEM((2, REACH, 8, 128), jnp.float32),
            pltpu.VMEM(tiles, jnp.bfloat16),
            pltpu.VMEM((REACH, 8, 128), jnp.float32),
            pltpu.VMEM(tiles, jnp.bfloat16),
            pltpu.VMEM((REACH, 8, 128), jnp.float32),
            pltpu.VMEM(tiles, jnp.bfloat16),
            pltpu.VMEM((REACH, 8, 128), jnp.float32),
            pltpu.VMEM((2, REQS, ROWS, HEAD), jnp.bfloat16),
            pltpu.VMEM((2, 8, 128), jnp.float32),
            pltpu.VMEM((REQS * ROWS, HEAD), jnp.float32),
            dma((2, REACH, 2)), dma((2, REACH, 2)), dma((1 + HALVES, REACH)), dma((1 + HALVES, REACH)),
            dma((1 + HALVES, 2)), dma((1 + HALVES, 2)),
        ],
        compiler_params=pltpu.CompilerParams(collective_id=2, has_side_effects=True, vmem_limit_bytes=16 * 2**20),
        name="gather",
    )(o, st)


def on_device(queries, new_keys, new_values, prefix_keys, prefix_values, prefix_block_scales,
              suffix_key_pools, suffix_value_pools, prefix_home, request_prefix, suffix_lengths, block_table):
    scales = jnp.swapaxes(prefix_block_scales, 1, 2)
    every, which, own_o, own_l, own_st, keys, values, key_scales, value_scales = spread(
        request_prefix, suffix_lengths, block_table, prefix_home, queries, prefix_keys, prefix_values,
        suffix_key_pools, suffix_value_pools, scales, new_keys, new_values)
    o, st = attend(which, every, own_o, own_l, own_st, key_scales, value_scales, keys, values)
    return gather(o, st)


def solution(mesh):
    return jax.shard_map(
        on_device,
        mesh=mesh,
        in_specs=(
            P(None, "group", None),
            P(None, "group", None),
            P(None, "group", None),
            P("group", "seq", None),
            P("group", "seq", None),
            P("group", "seq", None),
            P(("group", "seq"), None, None),
            P(("group", "seq"), None, None),
            P(),
            P("group"),
            P("group"),
            P("group", "seq", None),
        ),
        out_specs=P(None, "group", "seq"),
        check_vma=False,
    )
```

```python
import functools

import jax
import jax.numpy as jnp
from jax import lax
from jax.experimental import pallas as pl
from jax.experimental.pallas import tpu as pltpu
from jax.sharding import PartitionSpec as P

QUERY_HEADS = 64
KV_HEADS = 4
HEAD = 128
STEPS = 4
GROUP_HEADS = QUERY_HEADS // KV_HEADS
ROWS = STEPS * GROUP_HEADS
REACH = 3
X = 4
REQS = 4
ENTRIES = REACH * REQS
BLOCK = 128
PAGE = 64
LOG2E = 1.4426950408889634
LOWEST = -1e30
MESH = pl.DeviceIdType.MESH
VMEM = pltpu.VMEM
SMEM = pltpu.SMEM


def places():
    group, count = lax.axis_index("group"), lax.axis_size("group")
    seq = lax.axis_index("seq")
    core, z = lax.rem(seq, 2), seq // 2
    sibling = (group, z * 2 + (1 - core))
    across = (group, (1 - z) * 2 + core)

    def along(steps):
        passed = (lax.rem(group, X) + X + steps) // X - 1
        past = passed * passed
        return (lax.rem(group + count + steps, count), (z + past - 2 * z * past) * 2 + core)

    return seq, core, z, sibling, across, along


def remote(src, dst, send, recv, device):
    return pltpu.make_async_remote_copy(
        src_ref=src, dst_ref=dst, send_sem=send, recv_sem=recv, device_id=device, device_id_type=MESH
    )


PARTS = 2
FRESH = 128


def row_maker():
    eye = lax.broadcasted_iota(jnp.int32, (ROWS, 128), 0) == lax.broadcasted_iota(jnp.int32, (ROWS, 128), 1)

    def as_row(column):
        return jnp.sum(jnp.where(eye, column, 0.0), axis=0, keepdims=True)

    return as_row


def in_place(x):
    return pltpu.with_memory_space_constraint(x, pltpu.HBM)


def spread_kernel(prefix_hbm, length_hbm, table_hbm, home_hbm, scale_hbm, nk_hbm, nv_hbm,
                  q_hbm, k_hbm, v_hbm, kp_hbm, vp_hbm, all_ref, table_out, own_o, own_l, own_st, k_held, v_held, kscale, vscale,
                  prefix_ref, length_ref, table_ref, home_ref, scale_ref, nk_ref, nv_ref, s_sem,
                  own, raw, which_ref, rows, k_pages, v_pages, k_new, v_new, fresh, q_sem, h_sem, p_sem, x_send, x_recv,
                  w_send, w_recv, z_send, z_recv, c_send, c_recv, d_send, d_recv):
    seq, core, z, sibling, across, along = places()
    barrier = pltpu.get_barrier_semaphore()
    for device in (sibling, across, along(1), along(2)):
        pl.semaphore_signal(barrier, inc=1, device_id=device, device_id_type=MESH)
    fetch = pltpu.make_async_copy(q_hbm, own, q_sem)
    fetch.start()
    small = [pltpu.make_async_copy(src, dst, s_sem.at[i]) for i, (src, dst) in enumerate((
        (prefix_hbm, prefix_ref), (home_hbm, home_ref), (length_hbm, length_ref), (table_hbm, table_ref),
        (scale_hbm, scale_ref), (nk_hbm, nk_ref), (nv_hbm, nv_ref)))]
    for copy in small:
        copy.start()
    page_copies = [pltpu.make_async_copy(kp_hbm, k_pages, p_sem.at[0]), pltpu.make_async_copy(vp_hbm, v_pages, p_sem.at[1])]
    holds = []
    for i, (src, dst) in enumerate(((k_hbm, k_held), (v_hbm, v_held))):
        holds += [pltpu.make_async_copy(src.at[p], dst.at[p], h_sem.at[i, p]) for p in range(src.shape[0])]
    for copy in page_copies:
        copy.start()

    share = GROUP_HEADS * HEAD

    def lanes_of(c):
        return pl.ds(pl.multiple_of(c * share, share), share)

    fetch.wait()
    pl.semaphore_wait(barrier, 4)
    part = STEPS // PARTS
    order = [(j, p) for p in range(PARTS) for j in (2, 1)]
    arrivals = [(j, p) for p in range(PARTS) for j in (1, 2)]
    started, x_copies = [], {}
    for j, p in order:
        steps = pl.ds(p * part, part)
        there = lanes_of(along(-j)[1])
        x_copies[j, p] = remote(own.at[steps, :, there], raw.at[j - 1, steps, :, there],
                                x_send.at[j - 1, p], x_recv.at[j - 1, p], along(-j))
        x_copies[j, p].start()
        started.append(x_copies[j, p])
    for copy in small:
        copy.wait()
    lane = lax.broadcasted_iota(jnp.int32, (8, 128), 1)
    which = jnp.zeros((8, 128), jnp.int32)
    for r in range(REQS):
        which = jnp.where(lane == r, prefix_ref[r], which)
    which_ref[0] = which
    homes = jnp.zeros((8, 128), jnp.int32)
    for p in range(home_ref.shape[0]):
        homes = jnp.where(lane == p, home_ref[p], homes)
    notes = {}
    for j in (2, 1):
        notes[j] = remote(which_ref.at[0], which_ref.at[j], w_send.at[j - 1], w_recv.at[j - 1], along(-j))
        notes[j].start()
        started.append(notes[j])

    def reorder(source, j, c, p):
        for t in range(p * part, (p + 1) * part):
            for h in range(GROUP_HEADS):
                at = pl.ds(pl.multiple_of((c * GROUP_HEADS + h) * HEAD, HEAD), HEAD)
                rows[pl.ds(t * GROUP_HEADS + h, REQS, stride=ROWS), :] = source[t, :, at].astype(jnp.float32)
        lo, hi = p * part * GROUP_HEADS, (p + 1) * part * GROUP_HEADS
        for r in range(REQS):
            all_ref[j * REQS + r, c, lo:hi, :] = rows[r * ROWS + lo:r * ROWS + hi, :].astype(jnp.bfloat16)

    for copy in holds:
        copy.start()

    def reorder_own(c, carry):
        for p in range(PARTS):
            reorder(own, 0, c, p)
        return carry

    lax.fori_loop(0, KV_HEADS, reorder_own, 0)

    f32, bf16 = jnp.float32, jnp.bfloat16
    used, pages = STEPS * REQS, table_ref.shape[2]
    local = pages * PAGE
    for ref, new in ((k_new, nk_ref), (v_new, nv_ref)):
        for u in range(STEPS):
            fresh[u * REQS:(u + 1) * REQS, :] = new[u].astype(f32)
        ref[0:used, :] = fresh[...].astype(bf16)
        ref[used:, :] = jnp.zeros((FRESH - used, fresh.shape[1]), bf16)
    column = lax.broadcasted_iota(jnp.int32, (ROWS, local), 1)
    lane = lax.broadcasted_iota(jnp.int32, (ROWS, FRESH), 1)
    step = lax.broadcasted_iota(jnp.int32, (ROWS, FRESH), 0) // GROUP_HEADS
    older = (lane < (step + 1) * REQS) & (seq == 0)
    contract = (((1,), (1,)), ((), ()))
    as_row = row_maker()

    def suffix(r):
        seen = column < length_ref[r] - seq * local
        seen_new = older & (lax.rem(lane, REQS) == r)
        page = [table_ref[r, 0, b] for b in range(pages)]
        for c in range(KV_HEADS):
            lanes = slice(c * HEAD, (c + 1) * HEAD)
            k = jnp.concatenate([k_pages[p, :, lanes] for p in page], axis=0)
            v = jnp.concatenate([v_pages[p, :, lanes] for p in page], axis=0)
            q = all_ref[r, c]
            s_old = lax.dot_general(q, k, contract, preferred_element_type=f32) * (HEAD ** -0.5 * LOG2E)
            s_new = lax.dot_general(q, k_new[:, lanes], contract, preferred_element_type=f32) * (HEAD ** -0.5 * LOG2E)
            parts = [jnp.where(seen[:, i:i + FRESH], s_old[:, i:i + FRESH], LOWEST) for i in range(0, local, FRESH)]
            parts.append(jnp.where(seen_new, s_new, LOWEST))
            top = jnp.max(functools.reduce(jnp.maximum, parts), axis=1, keepdims=True)
            top = jnp.broadcast_to(top, (ROWS, FRESH))
            shown = [seen[:, i:i + FRESH] for i in range(0, local, FRESH)] + [seen_new]
            parts = [jnp.where(show, jnp.exp2(part - top), 0.0) for show, part in zip(shown, parts)]
            total = jnp.sum(functools.reduce(jnp.add, parts), axis=1, keepdims=True)
            total = jnp.broadcast_to(total, (ROWS, HEAD))
            acc = jnp.dot(jnp.concatenate(parts[:-1], axis=1).astype(bf16), v, preferred_element_type=f32)
            acc += jnp.dot(parts[-1].astype(bf16), v_new[:, lanes], preferred_element_type=f32)
            some = total > 0.0
            total = jnp.where(some, total, 1.0)
            lse = jnp.where(some, top + jnp.log2(total), LOWEST)
            own_o[c, r] = (acc / total).astype(bf16)
            own_l[c, r] = lse
            own_st[c, r:r + 1, :] = as_row(lse)

    blocks = k_held.shape[1] // BLOCK
    for s in range(k_held.shape[0]):
        x = scale_ref[s].astype(f32)
        x = jnp.concatenate([x, jnp.zeros((x.shape[0], 128 - blocks), f32)], axis=1).T[0:blocks]
        for c in range(KV_HEADS):
            kscale[s, c] = jnp.broadcast_to(x[:, c:c + 1] * (HEAD ** -0.5 * LOG2E), kscale.shape[2:])
            vscale[s, c] = jnp.broadcast_to(x[:, KV_HEADS + c:KV_HEADS + c + 1], vscale.shape[2:])
    for c in range(KV_HEADS):
        own_st[c] = jnp.full(own_st.shape[1:], LOWEST, f32)
    for copy in page_copies:
        copy.wait()
    for r in (0, 1, 2):
        suffix(r)

    beside = seq + 1 - 2 * core
    far, corner = lax.rem(seq + 2, 4), lax.rem(beside + 2, 4)

    def passed(j, p, c, send, recv, device):
        piece = raw.at[j - 1, pl.ds(p * part, part), :, lanes_of(c)]
        return remote(piece, piece, send.at[j - 1, p], recv.at[j - 1, p], device)

    for j, p in arrivals:
        passed(j, p, seq, x_send, x_recv, along(-j)).wait_recv()
        for copy in (passed(j, p, seq, z_send, z_recv, across), passed(j, p, seq, c_send, c_recv, sibling)):
            copy.start()
            started.append(copy)
    for j, p in arrivals:
        reorder(raw.at[j - 1], j, seq, p)
    suffix(3)
    for j, p in arrivals:
        passed(j, p, far, z_send, z_recv, across).wait_recv()
        copy = passed(j, p, far, d_send, d_recv, sibling)
        copy.start()
        started.append(copy)
    for j, p in arrivals:
        reorder(raw.at[j - 1], j, far, p)
    for j, p in arrivals:
        passed(j, p, beside, c_send, c_recv, sibling).wait_recv()
        reorder(raw.at[j - 1], j, beside, p)
    for j, p in arrivals:
        passed(j, p, corner, d_send, d_recv, sibling).wait_recv()
        reorder(raw.at[j - 1], j, corner, p)
    for j in (1, 2):
        notes[j].wait_recv()
    row = lax.broadcasted_iota(jnp.int32, (8, 128), 0)
    for j in range(REACH):
        homes = jnp.where(row == j, which_ref[j], homes)
    table_out[...] = homes
    for copy in started:
        copy.wait_send()
    for copy in holds:
        copy.wait()


def spread(request_prefix, lengths, table, home, queries, keys, values, key_pages, value_pages, scales, new_keys, new_values):
    dma = pltpu.SemaphoreType.DMA
    vmem, hbm = (pl.BlockSpec(memory_space=m) for m in (VMEM, pltpu.HBM))
    bf16, f32 = jnp.bfloat16, jnp.float32
    width = keys.shape[-1]
    small = (request_prefix, lengths, table, home)
    operands = small + (scales, new_keys, new_values, queries, keys, values, key_pages, value_pages)
    splat = (keys.shape[0], KV_HEADS, keys.shape[1] // BLOCK, 128)
    return pl.pallas_call(
        spread_kernel,
        out_shape=(
            pltpu.VMEM((ENTRIES, KV_HEADS, ROWS, HEAD), bf16),
            pltpu.VMEM((8, 128), jnp.int32),
            pltpu.VMEM((KV_HEADS, REQS, ROWS, HEAD), bf16),
            pltpu.VMEM((KV_HEADS, REQS, ROWS, HEAD), f32),
            pltpu.VMEM((KV_HEADS, 8, 128), f32),
            pltpu.VMEM(keys.shape, bf16),
            pltpu.VMEM(values.shape, bf16),
            pltpu.VMEM(splat, f32),
            pltpu.VMEM(splat, f32),
        ),
        in_specs=[hbm] * len(operands),
        out_specs=(vmem,) * 9,
        scratch_shapes=[pltpu.SMEM(x.shape, x.dtype) for x in small] + [
            pltpu.VMEM(scales.shape, bf16),
            pltpu.VMEM(new_keys.shape, bf16),
            pltpu.VMEM(new_values.shape, bf16),
            dma((7,)),
            pltpu.VMEM(queries.shape, bf16),
            pltpu.VMEM((2,) + queries.shape, bf16),
            pltpu.VMEM((REACH, 8, 128), jnp.int32),
            pltpu.VMEM((REQS * ROWS, HEAD), f32),
            pltpu.VMEM(key_pages.shape, bf16),
            pltpu.VMEM(value_pages.shape, bf16),
            pltpu.VMEM((FRESH, width), bf16),
            pltpu.VMEM((FRESH, width), bf16),
            pltpu.VMEM((STEPS * REQS, width), f32),
            dma, dma((2, 2)), dma((2,)), dma((2, PARTS)), dma((2, PARTS)), dma((2,)), dma((2,)),
            dma((2, PARTS)), dma((2, PARTS)), dma((2, PARTS)), dma((2, PARTS)), dma((2, PARTS)), dma((2, PARTS)),
        ],
        compiler_params=pltpu.CompilerParams(collective_id=1, has_side_effects=True, vmem_limit_bytes=14 * 2**20),
        name="spread",
    )(*map(in_place, operands))


GROUPED = 6
TILE = 256


def attend_kernel(which_ref, q_ref, own_o, own_l, own_st, kscale, vscale, kbuf, vbuf, o_ref, st_ref,
                  s_buf, jobs, counts):
    slots, span, _ = kbuf.shape
    me = lax.axis_index("group")
    f32, bf16 = jnp.float32, jnp.bfloat16

    found = [jnp.int32(0)] * slots
    for e in range(ENTRIES):
        row = which_ref[REACH, which_ref[e // REQS, e % REQS]]
        for s in range(slots):
            jobs[s, found[s]] = e
            found[s] += jnp.where(row == me * slots + s, 1, 0)
    for s in range(slots):
        counts[s] = found[s]

    o_ref[:, pl.ds(REQS, ENTRIES - REQS)] = jnp.zeros((KV_HEADS, ENTRIES - REQS, ROWS, HEAD), bf16)
    st_ref[...] = jnp.full(st_ref.shape, LOWEST, f32)

    as_row = row_maker()

    for c in range(KV_HEADS):
        for r in range(REQS):
            o_ref[c, r] = own_o[c, r]
        st_ref[c, 0] = own_st[c]

    per_tile = TILE // BLOCK
    tiles = span // TILE

    def group(s, at, n):
        rows = n * ROWS

        def lanes_of(c):
            return pl.ds(pl.multiple_of(c * HEAD, HEAD), HEAD)

        def queries_of(c):
            return jnp.concatenate([q_ref[jobs[s, at + j], c] for j in range(n)], axis=0)

        def score(buf, q, c, t, m):
            k = kbuf[s, t * TILE:(t + 1) * TILE, lanes_of(c)]
            sc = lax.dot_general(q, k, (((1,), (1,)), ((), ())), preferred_element_type=f32)
            for b in range(per_tile):
                part = sc[:, b * BLOCK:(b + 1) * BLOCK] * kscale[s, c, t * per_tile + b:t * per_tile + b + 1, :]
                buf[t * per_tile + b, 0:rows, :] = part
                m = jnp.maximum(m, part)
            return m

        def weigh(buf, top, c, t, total, acc):
            parts = []
            for b in range(per_tile):
                p = jnp.exp2(buf[t * per_tile + b, 0:rows, :] - top)
                total = total + p
                p = p * vscale[s, c, t * per_tile + b:t * per_tile + b + 1, :]
                parts.append(p.astype(bf16))
            v = vbuf[s, t * TILE:(t + 1) * TILE, lanes_of(c)]
            acc = acc + jnp.dot(jnp.concatenate(parts, axis=1), v, preferred_element_type=f32)
            return total, acc

        def row_top(m):
            return jnp.broadcast_to(jnp.max(m, axis=1, keepdims=True), (rows, HEAD))

        def finish(c, top, total, acc):
            total = jnp.broadcast_to(jnp.sum(total, axis=1, keepdims=True), (rows, HEAD))
            lse = top + jnp.log2(total)
            out = acc / total
            for j in range(n):
                e = jobs[s, at + j]
                mine = slice(j * ROWS, (j + 1) * ROWS)
                old = jnp.where(e < REQS, own_l[c, jnp.minimum(e, REQS - 1)], LOWEST)
                share = 1.0 / (1.0 + jnp.exp2(old - lse[mine]))
                before = o_ref[c, e].astype(f32)
                o_ref[c, e] = (before + share * (out[mine] - before)).astype(bf16)
                both = jnp.maximum(old, lse[mine]) + jnp.log2(1.0 + jnp.exp2(-jnp.abs(old - lse[mine])))
                st_ref[c, e // REQS, pl.ds(lax.rem(e, REQS), 1), :] = as_row(both)

        def weigh_and_score(c, top, following):
            q = queries_of(following) if following is not None else None
            m = jnp.full((rows, BLOCK), LOWEST, f32)
            total = jnp.zeros((rows, HEAD), f32)
            acc = jnp.zeros((rows, HEAD), f32)
            for t in range(tiles):
                total, acc = weigh(s_buf, top, c, t, total, acc)
                if following is not None:
                    m = score(s_buf, q, following, t, m)
            finish(c, top, total, acc)
            return row_top(m)

        q = queries_of(0)
        m = jnp.full((rows, BLOCK), LOWEST, f32)
        for t in range(tiles):
            m = score(s_buf, q, 0, t, m)
        top = lax.fori_loop(0, KV_HEADS - 1, lambda c, top: weigh_and_score(c, top, c + 1), row_top(m))
        weigh_and_score(KV_HEADS - 1, top, None)

    def one_slot(s, carry):
        wanted = counts[s]

        def some(i, carry):
            at = i * GROUPED
            left = jnp.minimum(wanted - at, GROUPED)
            for n in range(1, GROUPED + 1):
                @pl.when(left == n)
                def _(n=n):
                    group(s, at, n)
            return carry

        lax.fori_loop(0, (wanted + GROUPED - 1) // GROUPED, some, 0)
        return carry

    lax.fori_loop(0, slots, one_slot, 0)


def attend(which, q, own_o, own_l, own_st, key_scales, value_scales, k, v):
    slots, span, width = k.shape
    vmem, smem = (pl.BlockSpec(memory_space=m) for m in (VMEM, SMEM))
    return pl.pallas_call(
        attend_kernel,
        out_shape=(
            pltpu.VMEM((KV_HEADS, ENTRIES, ROWS, HEAD), jnp.bfloat16),
            pltpu.VMEM((KV_HEADS, REACH, 8, 128), jnp.float32),
        ),
        in_specs=[smem] + [vmem] * 8,
        out_specs=(vmem, vmem),
        scratch_shapes=[
            pltpu.VMEM((span // BLOCK, GROUPED * ROWS, BLOCK), jnp.float32),
            pltpu.SMEM((slots, 16), jnp.int32),
            pltpu.SMEM((slots,), jnp.int32),
        ],
        compiler_params=pltpu.CompilerParams(vmem_limit_bytes=24 * 2**20),
        name="attend",
    )(which, q, own_o, own_l, own_st, key_scales, value_scales, k, v)


HALVES = 2


def gather_kernel(o_ref, st_ref, out_ref, c_o, c_s, z_o, z_s, zr_o, zr_s, x_o, x_s, xr_o, xr_s, rows,
                  c_send, c_recv, z_send, z_recv, x_send, x_recv):
    seq, core, z, sibling, across, along = places()
    f32, bf16 = jnp.float32, jnp.bfloat16
    barrier = pltpu.get_barrier_semaphore()
    for device in (sibling, across, along(-1), along(-2)):
        pl.semaphore_signal(barrier, inc=1, device_id=device, device_id_type=MESH)
    pl.semaphore_wait(barrier, 4)

    def entries(j):
        return pl.ds(j * REQS, REQS)

    half = REQS // HALVES

    def half_of(j, p):
        return pl.ds(j * REQS + p * half, half)

    def joined(s1, s2):
        gap = s2 - s1
        share = 1.0 / (1.0 + jnp.exp2(gap))
        return share.T, jnp.maximum(s1, s2) + jnp.log2(1.0 + jnp.exp2(-jnp.abs(gap)))

    def mixed(share, i, first, second):
        second = second.astype(f32)
        return second + share[0:ROWS, i:i + 1] * (first.astype(f32) - second)

    order = (2, 1, 0)

    def kept(j):
        return along(j)[1] if j else seq

    def given(j):
        return lax.rem(kept(j) + 2, 4)

    core_copies, waits = {}, []
    for k in (0, 1):
        for j in order:
            head = (given(j) if k == 0 else kept(j)) + 1 - 2 * core
            core_copies[j, k] = (
                remote(o_ref.at[head, entries(j)], c_o.at[k, entries(j)], c_send.at[0, j, k], c_recv.at[0, j, k], sibling),
                remote(st_ref.at[head, j], c_s.at[k, j], c_send.at[1, j, k], c_recv.at[1, j, k], sibling),
            )
            for copy in core_copies[j, k]:
                copy.start()
                waits.append(copy)
    z_copies = {}
    for k in (0, 1):
        for j in order:
            for copy in core_copies[j, k]:
                copy.wait_recv()
            head = given(j) if k == 0 else kept(j)
            share, both = joined(st_ref[head, j], c_s[k, j])
            to_o, to_s = (z_o, z_s) if k == 0 else (x_o, x_s)
            to_s[j] = both
            if k == 0:
                z_copies[j] = [remote(z_s.at[j], zr_s.at[j], z_send.at[HALVES, j], z_recv.at[HALVES, j], across)]
                z_copies[j][0].start()
            for p in range(HALVES):
                for i in range(p * half, (p + 1) * half):
                    e = j * REQS + i
                    to_o[e] = mixed(share, i, o_ref[head, e], c_o[k, e]).astype(bf16)
                if k == 0:
                    copy = remote(z_o.at[half_of(j, p)], zr_o.at[half_of(j, p)], z_send.at[p, j], z_recv.at[p, j], across)
                    copy.start()
                    z_copies[j].append(copy)
            if k == 0:
                waits += z_copies[j]
    x_copies = {}
    for j in order:
        z_copies[j][0].wait_recv()
        share, both = joined(x_s[j], zr_s[j])
        x_s[j] = both
        if j:
            x_copies[j] = [remote(x_s.at[j], xr_s.at[j - 1], x_send.at[HALVES, j - 1], x_recv.at[HALVES, j - 1], along(j))]
            x_copies[j][0].start()
        for p in range(HALVES):
            z_copies[j][1 + p].wait_recv()
            for i in range(p * half, (p + 1) * half):
                e = j * REQS + i
                x_o[e] = mixed(share, i, x_o[e], zr_o[e]).astype(bf16)
            if j:
                copy = remote(x_o.at[half_of(j, p)], xr_o.at[j - 1, pl.ds(p * half, half)],
                              x_send.at[p, j - 1], x_recv.at[p, j - 1], along(j))
                copy.start()
                x_copies[j].append(copy)
        if j:
            waits += x_copies[j]
    for j in (1, 2):
        for copy in x_copies[j]:
            copy.wait_recv()
    share1, both = joined(x_s[0], xr_s[0])
    share2, _ = joined(both, xr_s[1])
    for i in range(REQS):
        part = mixed(share1, i, x_o[i], xr_o[0, i])
        rows[i * ROWS:(i + 1) * ROWS, :] = mixed(share2, i, part, xr_o[1, i])
    for t in range(STEPS):
        for h in range(GROUP_HEADS):
            tile = rows[pl.ds(t * GROUP_HEADS + h, REQS, stride=ROWS), :]
            out_ref[t, :, h * HEAD:(h + 1) * HEAD] = tile.astype(bf16)
    for copy in waits:
        copy.wait_send()


def gather(o, st):
    dma = pltpu.SemaphoreType.DMA
    vmem = pl.BlockSpec(memory_space=VMEM)
    tiles = (ENTRIES, ROWS, HEAD)
    return pl.pallas_call(
        gather_kernel,
        out_shape=jax.ShapeDtypeStruct((STEPS, REQS, GROUP_HEADS * HEAD), jnp.bfloat16),
        in_specs=[vmem, vmem],
        out_specs=vmem,
        scratch_shapes=[
            pltpu.VMEM((2,) + tiles, jnp.bfloat16),
            pltpu.VMEM((2, REACH, 8, 128), jnp.float32),
            pltpu.VMEM(tiles, jnp.bfloat16),
            pltpu.VMEM((REACH, 8, 128), jnp.float32),
            pltpu.VMEM(tiles, jnp.bfloat16),
            pltpu.VMEM((REACH, 8, 128), jnp.float32),
            pltpu.VMEM(tiles, jnp.bfloat16),
            pltpu.VMEM((REACH, 8, 128), jnp.float32),
            pltpu.VMEM((2, REQS, ROWS, HEAD), jnp.bfloat16),
            pltpu.VMEM((2, 8, 128), jnp.float32),
            pltpu.VMEM((REQS * ROWS, HEAD), jnp.float32),
            dma((2, REACH, 2)), dma((2, REACH, 2)), dma((1 + HALVES, REACH)), dma((1 + HALVES, REACH)),
            dma((1 + HALVES, 2)), dma((1 + HALVES, 2)),
        ],
        compiler_params=pltpu.CompilerParams(collective_id=2, has_side_effects=True, vmem_limit_bytes=16 * 2**20),
        name="gather",
    )(o, st)


def on_device(queries, new_keys, new_values, prefix_keys, prefix_values, prefix_block_scales,
              suffix_key_pools, suffix_value_pools, prefix_home, request_prefix, suffix_lengths, block_table):
    scales = jnp.swapaxes(prefix_block_scales, 1, 2)
    every, which, own_o, own_l, own_st, keys, values, key_scales, value_scales = spread(
        request_prefix, suffix_lengths, block_table, prefix_home, queries, prefix_keys, prefix_values,
        suffix_key_pools, suffix_value_pools, scales, new_keys, new_values)
    o, st = attend(which, every, own_o, own_l, own_st, key_scales, value_scales, keys, values)
    return gather(o, st)


def solution(mesh):
    return jax.shard_map(
        on_device,
        mesh=mesh,
        in_specs=(
            P(None, "group", None),
            P(None, "group", None),
            P(None, "group", None),
            P("group", "seq", None),
            P("group", "seq", None),
            P("group", "seq", None),
            P(("group", "seq"), None, None),
            P(("group", "seq"), None, None),
            P(),
            P("group"),
            P("group"),
            P("group", "seq", None),
        ),
        out_specs=P(None, "group", "seq"),
        check_vma=False,
    )
```

```python
import functools

import jax
import jax.numpy as jnp
from jax import lax
from jax.experimental import pallas as pl
from jax.experimental.pallas import tpu as pltpu
from jax.sharding import PartitionSpec as P

QUERY_HEADS = 64
KV_HEADS = 4
HEAD = 128
STEPS = 4
GROUP_HEADS = QUERY_HEADS // KV_HEADS
ROWS = STEPS * GROUP_HEADS
REACH = 3
X = 4
REQS = 4
ENTRIES = REACH * REQS
BLOCK = 128
PAGE = 64
LOG2E = 1.4426950408889634
LOWEST = -1e30
MESH = pl.DeviceIdType.MESH
VMEM = pltpu.VMEM
SMEM = pltpu.SMEM


def places():
    group, count = lax.axis_index("group"), lax.axis_size("group")
    seq = lax.axis_index("seq")
    core, z = lax.rem(seq, 2), seq // 2
    sibling = (group, z * 2 + (1 - core))
    across = (group, (1 - z) * 2 + core)

    def along(steps):
        passed = (lax.rem(group, X) + X + steps) // X - 1
        past = passed * passed
        return (lax.rem(group + count + steps, count), (z + past - 2 * z * past) * 2 + core)

    return seq, core, z, sibling, across, along


def remote(src, dst, send, recv, device):
    return pltpu.make_async_remote_copy(
        src_ref=src, dst_ref=dst, send_sem=send, recv_sem=recv, device_id=device, device_id_type=MESH
    )


PARTS = 2
FRESH = 128


def row_maker():
    eye = lax.broadcasted_iota(jnp.int32, (ROWS, 128), 0) == lax.broadcasted_iota(jnp.int32, (ROWS, 128), 1)

    def as_row(column):
        return jnp.sum(jnp.where(eye, column, 0.0), axis=0, keepdims=True)

    return as_row


def in_place(x):
    return pltpu.with_memory_space_constraint(x, pltpu.HBM)


def spread_kernel(prefix_hbm, length_hbm, table_hbm, home_hbm, scale_hbm, nk_hbm, nv_hbm,
                  q_hbm, k_hbm, v_hbm, kp_hbm, vp_hbm, all_ref, table_out, own_o, own_l, own_st, k_held, v_held, kscale, vscale,
                  prefix_ref, length_ref, table_ref, home_ref, scale_ref, nk_ref, nv_ref, s_sem,
                  own, raw, which_ref, rows, k_pages, v_pages, k_new, v_new, fresh, q_sem, h_sem, p_sem, x_send, x_recv,
                  w_send, w_recv, z_send, z_recv, c_send, c_recv, d_send, d_recv):
    seq, core, z, sibling, across, along = places()
    barrier = pltpu.get_barrier_semaphore()
    for device in (sibling, across, along(1), along(2)):
        pl.semaphore_signal(barrier, inc=1, device_id=device, device_id_type=MESH)
    fetch = pltpu.make_async_copy(q_hbm, own, q_sem)
    fetch.start()
    small = [pltpu.make_async_copy(src, dst, s_sem.at[i]) for i, (src, dst) in enumerate((
        (prefix_hbm, prefix_ref), (home_hbm, home_ref), (length_hbm, length_ref), (table_hbm, table_ref),
        (scale_hbm, scale_ref), (nk_hbm, nk_ref), (nv_hbm, nv_ref)))]
    for copy in small:
        copy.start()
    page_copies = [pltpu.make_async_copy(kp_hbm, k_pages, p_sem.at[0]), pltpu.make_async_copy(vp_hbm, v_pages, p_sem.at[1])]
    holds = []
    for i, (src, dst) in enumerate(((k_hbm, k_held), (v_hbm, v_held))):
        holds += [pltpu.make_async_copy(src.at[p], dst.at[p], h_sem.at[i, p]) for p in range(src.shape[0])]
    for copy in page_copies:
        copy.start()

    share = GROUP_HEADS * HEAD

    def lanes_of(c):
        return pl.ds(pl.multiple_of(c * share, share), share)

    fetch.wait()
    pl.semaphore_wait(barrier, 4)
    part = STEPS // PARTS
    order = [(j, p) for p in range(PARTS) for j in (2, 1)]
    arrivals = [(j, p) for p in range(PARTS) for j in (1, 2)]
    started, x_copies = [], {}
    for j, p in order:
        steps = pl.ds(p * part, part)
        there = lanes_of(along(-j)[1])
        x_copies[j, p] = remote(own.at[steps, :, there], raw.at[j - 1, steps, :, there],
                                x_send.at[j - 1, p], x_recv.at[j - 1, p], along(-j))
        x_copies[j, p].start()
        started.append(x_copies[j, p])
    for copy in small:
        copy.wait()
    lane = lax.broadcasted_iota(jnp.int32, (8, 128), 1)
    which = jnp.zeros((8, 128), jnp.int32)
    for r in range(REQS):
        which = jnp.where(lane == r, prefix_ref[r], which)
    which_ref[0] = which
    homes = jnp.zeros((8, 128), jnp.int32)
    for p in range(home_ref.shape[0]):
        homes = jnp.where(lane == p, home_ref[p], homes)
    notes = {}
    for j in (2, 1):
        notes[j] = remote(which_ref.at[0], which_ref.at[j], w_send.at[j - 1], w_recv.at[j - 1], along(-j))
        notes[j].start()
        started.append(notes[j])

    def reorder(source, j, c, p):
        for t in range(p * part, (p + 1) * part):
            for h in range(GROUP_HEADS):
                at = pl.ds(pl.multiple_of((c * GROUP_HEADS + h) * HEAD, HEAD), HEAD)
                rows[pl.ds(t * GROUP_HEADS + h, REQS, stride=ROWS), :] = source[t, :, at].astype(jnp.float32)
        lo, hi = p * part * GROUP_HEADS, (p + 1) * part * GROUP_HEADS
        for r in range(REQS):
            all_ref[j * REQS + r, c, lo:hi, :] = rows[r * ROWS + lo:r * ROWS + hi, :].astype(jnp.bfloat16)

    for copy in holds:
        copy.start()

    def reorder_own(c, carry):
        for p in range(PARTS):
            reorder(own, 0, c, p)
        return carry

    lax.fori_loop(0, KV_HEADS, reorder_own, 0)

    f32, bf16 = jnp.float32, jnp.bfloat16
    used, pages = STEPS * REQS, table_ref.shape[2]
    local = pages * PAGE
    for ref, new in ((k_new, nk_ref), (v_new, nv_ref)):
        for u in range(STEPS):
            fresh[u * REQS:(u + 1) * REQS, :] = new[u].astype(f32)
        ref[0:used, :] = fresh[...].astype(bf16)
        ref[used:, :] = jnp.zeros((FRESH - used, fresh.shape[1]), bf16)
    column = lax.broadcasted_iota(jnp.int32, (ROWS, local), 1)
    lane = lax.broadcasted_iota(jnp.int32, (ROWS, FRESH), 1)
    step = lax.broadcasted_iota(jnp.int32, (ROWS, FRESH), 0) // GROUP_HEADS
    older = (lane < (step + 1) * REQS) & (seq == 0)
    contract = (((1,), (1,)), ((), ()))
    as_row = row_maker()

    def suffix(r):
        seen = column < length_ref[r] - seq * local
        seen_new = older & (lax.rem(lane, REQS) == r)
        page = [table_ref[r, 0, b] for b in range(pages)]
        for c in range(KV_HEADS):
            lanes = slice(c * HEAD, (c + 1) * HEAD)
            k = jnp.concatenate([k_pages[p, :, lanes] for p in page], axis=0)
            v = jnp.concatenate([v_pages[p, :, lanes] for p in page], axis=0)
            q = all_ref[r, c]
            s_old = lax.dot_general(q, k, contract, preferred_element_type=f32) * (HEAD ** -0.5 * LOG2E)
            s_new = lax.dot_general(q, k_new[:, lanes], contract, preferred_element_type=f32) * (HEAD ** -0.5 * LOG2E)
            parts = [jnp.where(seen[:, i:i + FRESH], s_old[:, i:i + FRESH], LOWEST) for i in range(0, local, FRESH)]
            parts.append(jnp.where(seen_new, s_new, LOWEST))
            top = jnp.max(functools.reduce(jnp.maximum, parts), axis=1, keepdims=True)
            top = jnp.broadcast_to(top, (ROWS, FRESH))
            shown = [seen[:, i:i + FRESH] for i in range(0, local, FRESH)] + [seen_new]
            parts = [jnp.where(show, jnp.exp2(part - top), 0.0) for show, part in zip(shown, parts)]
            total = jnp.sum(functools.reduce(jnp.add, parts), axis=1, keepdims=True)
            total = jnp.broadcast_to(total, (ROWS, HEAD))
            acc = jnp.dot(jnp.concatenate(parts[:-1], axis=1).astype(bf16), v, preferred_element_type=f32)
            acc += jnp.dot(parts[-1].astype(bf16), v_new[:, lanes], preferred_element_type=f32)
            some = total > 0.0
            total = jnp.where(some, total, 1.0)
            lse = jnp.where(some, top + jnp.log2(total), LOWEST)
            own_o[c, r] = (acc / total).astype(bf16)
            own_l[c, r] = lse
            own_st[c, r:r + 1, :] = as_row(lse)

    blocks = k_held.shape[1] // BLOCK
    for s in range(k_held.shape[0]):
        x = scale_ref[s].astype(f32)
        x = jnp.concatenate([x, jnp.zeros((x.shape[0], 128 - blocks), f32)], axis=1).T[0:blocks]
        for c in range(KV_HEADS):
            kscale[s, c] = jnp.broadcast_to(x[:, c:c + 1] * (HEAD ** -0.5 * LOG2E), kscale.shape[2:])
            vscale[s, c] = jnp.broadcast_to(x[:, KV_HEADS + c:KV_HEADS + c + 1], vscale.shape[2:])
    for c in range(KV_HEADS):
        own_st[c] = jnp.full(own_st.shape[1:], LOWEST, f32)
    for copy in page_copies:
        copy.wait()
    for r in range(REQS):
        suffix(r)

    beside = seq + 1 - 2 * core
    far, corner = lax.rem(seq + 2, 4), lax.rem(beside + 2, 4)

    def passed(j, p, c, send, recv, device):
        piece = raw.at[j - 1, pl.ds(p * part, part), :, lanes_of(c)]
        return remote(piece, piece, send.at[j - 1, p], recv.at[j - 1, p], device)

    for j, p in arrivals:
        passed(j, p, seq, x_send, x_recv, along(-j)).wait_recv()
        for copy in (passed(j, p, seq, z_send, z_recv, across), passed(j, p, seq, c_send, c_recv, sibling)):
            copy.start()
            started.append(copy)
    for j, p in arrivals:
        reorder(raw.at[j - 1], j, seq, p)
    for j, p in arrivals:
        passed(j, p, far, z_send, z_recv, across).wait_recv()
        copy = passed(j, p, far, d_send, d_recv, sibling)
        copy.start()
        started.append(copy)
    for j, p in arrivals:
        reorder(raw.at[j - 1], j, far, p)
    for j, p in arrivals:
        passed(j, p, beside, c_send, c_recv, sibling).wait_recv()
        reorder(raw.at[j - 1], j, beside, p)
    for j, p in arrivals:
        passed(j, p, corner, d_send, d_recv, sibling).wait_recv()
        reorder(raw.at[j - 1], j, corner, p)
    for j in (1, 2):
        notes[j].wait_recv()
    row = lax.broadcasted_iota(jnp.int32, (8, 128), 0)
    for j in range(REACH):
        homes = jnp.where(row == j, which_ref[j], homes)
    table_out[...] = homes
    for copy in started:
        copy.wait_send()
    for copy in holds:
        copy.wait()


def spread(request_prefix, lengths, table, home, queries, keys, values, key_pages, value_pages, scales, new_keys, new_values):
    dma = pltpu.SemaphoreType.DMA
    vmem, hbm = (pl.BlockSpec(memory_space=m) for m in (VMEM, pltpu.HBM))
    bf16, f32 = jnp.bfloat16, jnp.float32
    width = keys.shape[-1]
    small = (request_prefix, lengths, table, home)
    operands = small + (scales, new_keys, new_values, queries, keys, values, key_pages, value_pages)
    splat = (keys.shape[0], KV_HEADS, keys.shape[1] // BLOCK, 128)
    return pl.pallas_call(
        spread_kernel,
        out_shape=(
            pltpu.VMEM((ENTRIES, KV_HEADS, ROWS, HEAD), bf16),
            pltpu.VMEM((8, 128), jnp.int32),
            pltpu.VMEM((KV_HEADS, REQS, ROWS, HEAD), bf16),
            pltpu.VMEM((KV_HEADS, REQS, ROWS, HEAD), f32),
            pltpu.VMEM((KV_HEADS, 8, 128), f32),
            pltpu.VMEM(keys.shape, bf16),
            pltpu.VMEM(values.shape, bf16),
            pltpu.VMEM(splat, f32),
            pltpu.VMEM(splat, f32),
        ),
        in_specs=[hbm] * len(operands),
        out_specs=(vmem,) * 9,
        scratch_shapes=[pltpu.SMEM(x.shape, x.dtype) for x in small] + [
            pltpu.VMEM(scales.shape, bf16),
            pltpu.VMEM(new_keys.shape, bf16),
            pltpu.VMEM(new_values.shape, bf16),
            dma((7,)),
            pltpu.VMEM(queries.shape, bf16),
            pltpu.VMEM((2,) + queries.shape, bf16),
            pltpu.VMEM((REACH, 8, 128), jnp.int32),
            pltpu.VMEM((REQS * ROWS, HEAD), f32),
            pltpu.VMEM(key_pages.shape, bf16),
            pltpu.VMEM(value_pages.shape, bf16),
            pltpu.VMEM((FRESH, width), bf16),
            pltpu.VMEM((FRESH, width), bf16),
            pltpu.VMEM((STEPS * REQS, width), f32),
            dma, dma((2, 2)), dma((2,)), dma((2, PARTS)), dma((2, PARTS)), dma((2,)), dma((2,)),
            dma((2, PARTS)), dma((2, PARTS)), dma((2, PARTS)), dma((2, PARTS)), dma((2, PARTS)), dma((2, PARTS)),
        ],
        compiler_params=pltpu.CompilerParams(collective_id=1, has_side_effects=True, vmem_limit_bytes=14 * 2**20),
        name="spread",
    )(*map(in_place, operands))


GROUPED = 6
TILE = 256


def attend_kernel(which_ref, q_ref, own_o, own_l, own_st, kscale, vscale, kbuf, vbuf, o_ref, st_ref,
                  s_buf, jobs, counts):
    slots, span, _ = kbuf.shape
    me = lax.axis_index("group")
    f32, bf16 = jnp.float32, jnp.bfloat16

    found = [jnp.int32(0)] * slots
    for e in range(ENTRIES):
        row = which_ref[REACH, which_ref[e // REQS, e % REQS]]
        for s in range(slots):
            jobs[s, found[s]] = e
            found[s] += jnp.where(row == me * slots + s, 1, 0)
    for s in range(slots):
        counts[s] = found[s]

    o_ref[:, pl.ds(REQS, ENTRIES - REQS)] = jnp.zeros((KV_HEADS, ENTRIES - REQS, ROWS, HEAD), bf16)
    st_ref[...] = jnp.full(st_ref.shape, LOWEST, f32)

    as_row = row_maker()

    for c in range(KV_HEADS):
        for r in range(REQS):
            o_ref[c, r] = own_o[c, r]
        st_ref[c, 0] = own_st[c]

    per_tile = TILE // BLOCK
    tiles = span // TILE

    def group(s, at, n):
        rows = n * ROWS

        def lanes_of(c):
            return pl.ds(pl.multiple_of(c * HEAD, HEAD), HEAD)

        def queries_of(c):
            return jnp.concatenate([q_ref[jobs[s, at + j], c] for j in range(n)], axis=0)

        def score(buf, q, c, t, m):
            k = kbuf[s, t * TILE:(t + 1) * TILE, lanes_of(c)]
            sc = lax.dot_general(q, k, (((1,), (1,)), ((), ())), preferred_element_type=f32)
            for b in range(per_tile):
                part = sc[:, b * BLOCK:(b + 1) * BLOCK] * kscale[s, c, t * per_tile + b:t * per_tile + b + 1, :]
                buf[t * per_tile + b, 0:rows, :] = part
                m = jnp.maximum(m, part)
            return m

        def weigh(buf, top, c, t, total, acc):
            parts = []
            for b in range(per_tile):
                p = jnp.exp2(buf[t * per_tile + b, 0:rows, :] - top)
                total = total + p
                p = p * vscale[s, c, t * per_tile + b:t * per_tile + b + 1, :]
                parts.append(p.astype(bf16))
            v = vbuf[s, t * TILE:(t + 1) * TILE, lanes_of(c)]
            acc = acc + jnp.dot(jnp.concatenate(parts, axis=1), v, preferred_element_type=f32)
            return total, acc

        def row_top(m):
            return jnp.broadcast_to(jnp.max(m, axis=1, keepdims=True), (rows, HEAD))

        def finish(c, top, total, acc):
            total = jnp.broadcast_to(jnp.sum(total, axis=1, keepdims=True), (rows, HEAD))
            lse = top + jnp.log2(total)
            out = acc / total
            for j in range(n):
                e = jobs[s, at + j]
                mine = slice(j * ROWS, (j + 1) * ROWS)
                old = jnp.where(e < REQS, own_l[c, jnp.minimum(e, REQS - 1)], LOWEST)
                share = 1.0 / (1.0 + jnp.exp2(old - lse[mine]))
                before = o_ref[c, e].astype(f32)
                o_ref[c, e] = (before + share * (out[mine] - before)).astype(bf16)
                both = jnp.maximum(old, lse[mine]) + jnp.log2(1.0 + jnp.exp2(-jnp.abs(old - lse[mine])))
                st_ref[c, e // REQS, pl.ds(lax.rem(e, REQS), 1), :] = as_row(both)

        def weigh_and_score(c, top, following):
            q = queries_of(following) if following is not None else None
            m = jnp.full((rows, BLOCK), LOWEST, f32)
            total = jnp.zeros((rows, HEAD), f32)
            acc = jnp.zeros((rows, HEAD), f32)
            for t in range(tiles):
                total, acc = weigh(s_buf, top, c, t, total, acc)
                if following is not None:
                    m = score(s_buf, q, following, t, m)
            finish(c, top, total, acc)
            return row_top(m)

        q = queries_of(0)
        m = jnp.full((rows, BLOCK), LOWEST, f32)
        for t in range(tiles):
            m = score(s_buf, q, 0, t, m)
        top = lax.fori_loop(0, KV_HEADS - 1, lambda c, top: weigh_and_score(c, top, c + 1), row_top(m))
        weigh_and_score(KV_HEADS - 1, top, None)

    def one_slot(s, carry):
        wanted = counts[s]

        def some(i, carry):
            at = i * GROUPED
            left = jnp.minimum(wanted - at, GROUPED)
            for n in range(1, GROUPED + 1):
                @pl.when(left == n)
                def _(n=n):
                    group(s, at, n)
            return carry

        lax.fori_loop(0, (wanted + GROUPED - 1) // GROUPED, some, 0)
        return carry

    lax.fori_loop(0, slots, one_slot, 0)


def attend(which, q, own_o, own_l, own_st, key_scales, value_scales, k, v):
    slots, span, width = k.shape
    vmem, smem = (pl.BlockSpec(memory_space=m) for m in (VMEM, SMEM))
    return pl.pallas_call(
        attend_kernel,
        out_shape=(
            pltpu.VMEM((KV_HEADS, ENTRIES, ROWS, HEAD), jnp.bfloat16),
            pltpu.VMEM((KV_HEADS, REACH, 8, 128), jnp.float32),
        ),
        in_specs=[smem] + [vmem] * 8,
        out_specs=(vmem, vmem),
        scratch_shapes=[
            pltpu.VMEM((span // BLOCK, GROUPED * ROWS, BLOCK), jnp.float32),
            pltpu.SMEM((slots, 16), jnp.int32),
            pltpu.SMEM((slots,), jnp.int32),
        ],
        compiler_params=pltpu.CompilerParams(vmem_limit_bytes=24 * 2**20),
        name="attend",
    )(which, q, own_o, own_l, own_st, key_scales, value_scales, k, v)


HALVES = 2


def gather_kernel(o_ref, st_ref, out_ref, c_o, c_s, z_o, z_s, zr_o, zr_s, x_o, x_s, xr_o, xr_s, rows,
                  c_send, c_recv, z_send, z_recv, x_send, x_recv):
    seq, core, z, sibling, across, along = places()
    f32, bf16 = jnp.float32, jnp.bfloat16
    barrier = pltpu.get_barrier_semaphore()
    for device in (sibling, across, along(-1), along(-2)):
        pl.semaphore_signal(barrier, inc=1, device_id=device, device_id_type=MESH)
    pl.semaphore_wait(barrier, 4)

    def entries(j):
        return pl.ds(j * REQS, REQS)

    half = REQS // HALVES

    def half_of(j, p):
        return pl.ds(j * REQS + p * half, half)

    def joined(s1, s2):
        gap = s2 - s1
        share = 1.0 / (1.0 + jnp.exp2(gap))
        return share.T, jnp.maximum(s1, s2) + jnp.log2(1.0 + jnp.exp2(-jnp.abs(gap)))

    def mixed(share, i, first, second):
        second = second.astype(f32)
        return second + share[0:ROWS, i:i + 1] * (first.astype(f32) - second)

    order = (2, 1, 0)

    def kept(j):
        return along(j)[1] if j else seq

    def given(j):
        return lax.rem(kept(j) + 2, 4)

    core_copies, waits = {}, []
    for k in (0, 1):
        for j in order:
            head = (given(j) if k == 0 else kept(j)) + 1 - 2 * core
            core_copies[j, k] = (
                remote(o_ref.at[head, entries(j)], c_o.at[k, entries(j)], c_send.at[0, j, k], c_recv.at[0, j, k], sibling),
                remote(st_ref.at[head, j], c_s.at[k, j], c_send.at[1, j, k], c_recv.at[1, j, k], sibling),
            )
            for copy in core_copies[j, k]:
                copy.start()
                waits.append(copy)
    z_copies = {}
    for k in (0, 1):
        for j in order:
            for copy in core_copies[j, k]:
                copy.wait_recv()
            head = given(j) if k == 0 else kept(j)
            share, both = joined(st_ref[head, j], c_s[k, j])
            to_o, to_s = (z_o, z_s) if k == 0 else (x_o, x_s)
            to_s[j] = both
            if k == 0:
                z_copies[j] = [remote(z_s.at[j], zr_s.at[j], z_send.at[HALVES, j], z_recv.at[HALVES, j], across)]
                z_copies[j][0].start()
            for p in range(HALVES):
                for i in range(p * half, (p + 1) * half):
                    e = j * REQS + i
                    to_o[e] = mixed(share, i, o_ref[head, e], c_o[k, e]).astype(bf16)
                if k == 0:
                    copy = remote(z_o.at[half_of(j, p)], zr_o.at[half_of(j, p)], z_send.at[p, j], z_recv.at[p, j], across)
                    copy.start()
                    z_copies[j].append(copy)
            if k == 0:
                waits += z_copies[j]
    x_copies = {}
    for j in order:
        z_copies[j][0].wait_recv()
        share, both = joined(x_s[j], zr_s[j])
        x_s[j] = both
        if j:
            x_copies[j] = [remote(x_s.at[j], xr_s.at[j - 1], x_send.at[HALVES, j - 1], x_recv.at[HALVES, j - 1], along(j))]
            x_copies[j][0].start()
        for p in range(HALVES):
            z_copies[j][1 + p].wait_recv()
            for i in range(p * half, (p + 1) * half):
                e = j * REQS + i
                x_o[e] = mixed(share, i, x_o[e], zr_o[e]).astype(bf16)
            if j:
                copy = remote(x_o.at[half_of(j, p)], xr_o.at[j - 1, pl.ds(p * half, half)],
                              x_send.at[p, j - 1], x_recv.at[p, j - 1], along(j))
                copy.start()
                x_copies[j].append(copy)
        if j:
            waits += x_copies[j]
    for j in (1, 2):
        for copy in x_copies[j]:
            copy.wait_recv()
    share1, both = joined(x_s[0], xr_s[0])
    share2, _ = joined(both, xr_s[1])
    for i in range(REQS):
        part = mixed(share1, i, x_o[i], xr_o[0, i])
        rows[i * ROWS:(i + 1) * ROWS, :] = mixed(share2, i, part, xr_o[1, i])
    for t in range(STEPS):
        for h in range(GROUP_HEADS):
            tile = rows[pl.ds(t * GROUP_HEADS + h, REQS, stride=ROWS), :]
            out_ref[t, :, h * HEAD:(h + 1) * HEAD] = tile.astype(bf16)
    for copy in waits:
        copy.wait_send()


def gather(o, st):
    dma = pltpu.SemaphoreType.DMA
    vmem = pl.BlockSpec(memory_space=VMEM)
    tiles = (ENTRIES, ROWS, HEAD)
    return pl.pallas_call(
        gather_kernel,
        out_shape=jax.ShapeDtypeStruct((STEPS, REQS, GROUP_HEADS * HEAD), jnp.bfloat16),
        in_specs=[vmem, vmem],
        out_specs=vmem,
        scratch_shapes=[
            pltpu.VMEM((2,) + tiles, jnp.bfloat16),
            pltpu.VMEM((2, REACH, 8, 128), jnp.float32),
            pltpu.VMEM(tiles, jnp.bfloat16),
            pltpu.VMEM((REACH, 8, 128), jnp.float32),
            pltpu.VMEM(tiles, jnp.bfloat16),
            pltpu.VMEM((REACH, 8, 128), jnp.float32),
            pltpu.VMEM(tiles, jnp.bfloat16),
            pltpu.VMEM((REACH, 8, 128), jnp.float32),
            pltpu.VMEM((2, REQS, ROWS, HEAD), jnp.bfloat16),
            pltpu.VMEM((2, 8, 128), jnp.float32),
            pltpu.VMEM((REQS * ROWS, HEAD), jnp.float32),
            dma((2, REACH, 2)), dma((2, REACH, 2)), dma((1 + HALVES, REACH)), dma((1 + HALVES, REACH)),
            dma((1 + HALVES, 2)), dma((1 + HALVES, 2)),
        ],
        compiler_params=pltpu.CompilerParams(collective_id=2, has_side_effects=True, vmem_limit_bytes=16 * 2**20),
        name="gather",
    )(o, st)


def on_device(queries, new_keys, new_values, prefix_keys, prefix_values, prefix_block_scales,
              suffix_key_pools, suffix_value_pools, prefix_home, request_prefix, suffix_lengths, block_table):
    scales = jnp.swapaxes(prefix_block_scales, 1, 2)
    every, which, own_o, own_l, own_st, keys, values, key_scales, value_scales = spread(
        request_prefix, suffix_lengths, block_table, prefix_home, queries, prefix_keys, prefix_values,
        suffix_key_pools, suffix_value_pools, scales, new_keys, new_values)
    o, st = attend(which, every, own_o, own_l, own_st, key_scales, value_scales, keys, values)
    return gather(o, st)


def solution(mesh):
    return jax.shard_map(
        on_device,
        mesh=mesh,
        in_specs=(
            P(None, "group", None),
            P(None, "group", None),
            P(None, "group", None),
            P("group", "seq", None),
            P("group", "seq", None),
            P("group", "seq", None),
            P(("group", "seq"), None, None),
            P(("group", "seq"), None, None),
            P(),
            P("group"),
            P("group"),
            P("group", "seq", None),
        ),
        out_specs=P(None, "group", "seq"),
        check_vma=False,
    )
```
